32 devices in a mesh: groups: 2 (over x), ctx: 16 (over z, y, core).
Axes of the slice: x: 2, y: 2, z: 4, core: 2. Of those that a mesh axis runs over, the one named last changes fastest.
Arguments:
- query: bfloat16 [8192, 1024], P(('groups', 'ctx')), parts along dimension 0, may hold values from -130 to 130, as said below
- key: bfloat16 [8192, 1024], P(('groups', 'ctx')), parts along dimension 0, may hold values from -4.5 to 4.5
- value: bfloat16 [8192, 1024], P(('groups', 'ctx')), parts along dimension 0, may hold values from -6 to 6
- cotangent: bfloat16 [8192, 1024], P(('groups', 'ctx')), parts along dimension 0, may hold values from -6 to 6
- global_ids: int32 [4], P('groups'), parts along dimension 0, may hold values from 0 to 63
- rand_owner: int32 [128, 6], P('groups'), parts along dimension 0, may hold values from 0 to 15, all different within a row; in each aligned block of 4 rows (0 to 3, 4 to 7, ...) at most 2 rows name the same one
- rand_local: int32 [128, 6], P('groups'), parts along dimension 0, may hold values from 0 to 3
Outputs:
- attended: bfloat16 [8192, 1024], P(('groups', 'ctx')), parts along dimension 0
- grad_query: bfloat16 [8192, 1024], P(('groups', 'ctx')), parts along dimension 0
- grad_key: bfloat16 [8192, 1024], P(('groups', 'ctx')), parts along dimension 0
- grad_value: bfloat16 [8192, 1024], P(('groups', 'ctx')), parts along dimension 0
The draws below stay inside these ranges and needn't reach their ends.
There are 2 independent parts, one for each index of `groups`. The reference program is written for one: setup_inputs(seed, part) draws one part's arguments, and reference() takes and returns one part's arrays. A program takes and returns all parts, laid end to end along the dimension named above; each array names one. Nothing has to cross between parts.
Inputs may be any that keep to these rules, and one draw needn't show every extreme that they name: query and key are drawn together. `rand_owner`: each row names 6 different devices. In the 4 rows of one device no device is named more than 2 times, and in some device's rows some device is named exactly 2 times.
All inputs are finite; a program needn't handle non-finite values.
Results may differ from the reference program's by a relative error of at most 0.017.
Values may be sent and summed in bfloat16 or wider, within the bound.
No kernel may reach another device: no remote copies, remote signals or barrier semaphores. Data moves between devices by JAX's collectives and lax.ppermute only.
A program may use at most 192 MiB of HBM per device.

```python
import math
import jax
import jax.numpy as jnp
import numpy as np
from jax import lax

HEAD_DIM = 64
HEADS = 16
GROUP_HEADS = 8
BLOCK = 64
GLOBALS = 2
ROUNDS = 3
BLK_DEV = 4
FEAT = 1024
HG = 2
NB = 64
TOKENS = 4096
SLOT = 2
N_CTX = 16


def paired_draw(base_key):
    mixed = jax.random.fold_in(base_key, 4021)
    first, second = jax.random.split(mixed, 2)
    shape = (TOKENS, HEADS * HEAD_DIM)
    key_part = jnp.clip(jax.random.normal(first, shape, jnp.float32), -4.0, 4.0)
    query_part = jnp.clip(jax.random.normal(second, shape, jnp.float32), -4.0, 4.0)
    return (query_part, key_part)


def draw_query(key, part):
    return paired_draw(key)[0].astype(jnp.bfloat16)


def draw_key(key, part):
    return paired_draw(key)[1].astype(jnp.bfloat16)


def set_ends(array, own_key, least, high):
    longest = array.shape.index(max(array.shape))
    spots = []
    for shift in (0, 1):
        where = [jax.random.randint(jax.random.fold_in(own_key, axis), (), 0, length) for axis, length in enumerate(array.shape)]
        where[longest] = (where[longest] + shift) % array.shape[longest]
        spots.append(tuple(where))
    return array.at[spots[0]].set(least).at[spots[1]].set(high)


def steps_of(stream_key, dims, pieces, low, top_value):
    def one(dim, shards_of):
        steps = jax.random.uniform(jax.random.fold_in(jax.random.fold_in(stream_key, 6), dim), (shards_of,), jnp.float32, low / len(pieces), top_value / len(pieces))
        return jnp.repeat(jnp.exp(steps), dims[dim] // shards_of).reshape((-1,) + (1,) * (len(dims) - dim - 1))

    level = one(*pieces[0])
    for cut in pieces[1:]:
        level = level * one(*cut)
    return level


def shared_out(own_key, own, number, rows, count, top, reach, skew):
    ranking = jax.random.permutation(own_key, count)
    heavy_load, ordinary = portions_of(count, rows * top, reach, skew, True), portions_of(count, rows * top, reach, skew, False)
    places = jnp.arange(count)

    def named(sizes, rotation):
        used = int((sizes > 0).sum())
        fixed = max(1, used // 4)
        moved = fixed + (places - fixed + rotation * (used - fixed)) % max(1, count - fixed)
        return jnp.zeros((count,), jnp.int32).at[ranking[jnp.where(places < fixed, places, moved)]].set(jnp.asarray(sizes, jnp.int32))

    sizes = jnp.where(number % 4 == 0, named(heavy_load, number // 4), named(ordinary, number - number // 4 - 1))
    mixed = jax.random.permutation(jax.random.fold_in(own, 3), count)
    giver, sink = mixed[0:count // 2 * 2:2], mixed[1:count // 2 * 2:2]
    slack = jnp.minimum(sizes[giver] - 1, reach - sizes[sink]) // 2
    slack = jnp.where((giver == ranking[0]) | (sink == ranking[0]) | (sizes[sink] == 0), 0, jnp.maximum(slack, 0))
    moved = jax.random.randint(jax.random.fold_in(own, 4), (count // 2,), 0, 1 << 20) % (slack + 1)
    sizes = sizes.at[giver].add(-moved).at[sink].add(moved)
    items = jnp.searchsorted(jnp.cumsum(sizes), jnp.arange(rows * top), side="right").astype(jnp.int32)
    listing = items.reshape(top, rows).T
    listing = listing[jax.random.permutation(jax.random.fold_in(own, 1), rows)]
    rotation = jax.random.randint(jax.random.fold_in(own, 2), (rows, 1), 0, top)
    return jnp.take_along_axis(listing, (jnp.arange(top)[None, :] + rotation) % top, axis=1)


def portions_of(count, total, most, skew, full):
    portions = [(1 << 20) // math.isqrt(rank ** skew) + 1 for rank in range(1, count + 1)]
    largest = most if full else min(most, max(-(-total // count), total * portions[0] // sum(portions)))
    least = 1 if total - largest >= count - 1 else 0
    holding, rest = [largest] + [least] * (count - 1), total - largest - least * (count - 1)
    while rest > 0:
        candidates = [i for i in range(1, count) if holding[i] < largest] or [i for i in range(1, count) if holding[i] < most]
        pool, remaining = sum([portions[i] for i in candidates]), rest
        for i in candidates:
            extra = min(most - holding[i], max(1, remaining * portions[i] // pool), rest)
            holding[i] = holding[i] + extra
            rest = rest - extra
    return np.array(holding)


def bell_draw(rng, shape, width, bound, pieces=(), held_as=jnp.bfloat16):
    factor_of = steps_of(rng, shape, pieces, -0.22, 0.18) if pieces else 1.0
    values = jax.random.normal(rng, shape, jnp.float32) * width * factor_of
    return jnp.minimum(jnp.maximum(values, -bound), bound).astype(held_as)


def setup_inputs(seed: int = 0, part: int = 0) -> dict:
    arg_keys = jax.random.split(jax.random.key(seed), 8)
    own_keys = jax.random.split(jax.random.fold_in(arg_keys[7], part), 8)
    query = draw_query(jax.random.fold_in(jax.random.fold_in(arg_keys[7], part), 71), part)
    key = draw_key(jax.random.fold_in(jax.random.fold_in(arg_keys[7], part), 71), part)
    value = bell_draw(own_keys[2], (TOKENS, FEAT), 1.0, 6.0, ((0, 16),))
    cotangent = bell_draw(own_keys[3], (TOKENS, FEAT), 1.0, 6.0, ((0, 16),))
    global_ids = jax.random.randint(own_keys[4], (GLOBALS,), 0, NB).astype(jnp.int32)
    rand_owner_keys = jax.random.split(jax.random.fold_in(own_keys[5], 1), NB // BLK_DEV)
    rand_owner_turns = jax.random.permutation(jax.random.fold_in(own_keys[5], 3), NB // BLK_DEV)
    rand_owner = jax.vmap(lambda own, number: shared_out(jax.random.fold_in(own_keys[5], 2), own, number, BLK_DEV, N_CTX, HG * ROUNDS, SLOT, 2))(rand_owner_keys, rand_owner_turns).reshape((NB, HG * ROUNDS))
    rand_local = set_ends(jax.random.randint(own_keys[6], (NB, HG * ROUNDS), 0, BLK_DEV), jax.random.fold_in(own_keys[6], 1), 0, BLK_DEV - 1).astype(jnp.int32)
    return dict(query=query, key=key, value=value, cotangent=cotangent, global_ids=global_ids, rand_owner=rand_owner, rand_local=rand_local)


NEG_FILL = -1.0e30


def reference(query, key, value, cotangent, global_ids, rand_owner, rand_local):
    features = HEADS * HEAD_DIM
    groups = HEADS // GROUP_HEADS
    key_kinds = 3 + GLOBALS + ROUNDS
    key_span = key_kinds * BLOCK
    score_scale = HEAD_DIM ** -0.5
    query_five = query.reshape(NB, BLOCK, groups, GROUP_HEADS, HEAD_DIM)
    key_five = key.reshape(NB, BLOCK, groups, GROUP_HEADS, HEAD_DIM)
    value_five = value.reshape(NB, BLOCK, groups, GROUP_HEADS, HEAD_DIM)
    cot_five = cotangent.reshape(NB, BLOCK, groups, GROUP_HEADS, HEAD_DIM)
    rand_ids = (rand_owner * BLK_DEV + rand_local).astype(jnp.int32).reshape(NB, groups, ROUNDS)
    glob_ids = global_ids.astype(jnp.int32)
    group_col = jnp.arange(groups, dtype=jnp.int32)[:, None]

    def one_block(grad_pair, block_index):
        grad_k, grad_v = grad_pair
        window_raw = block_index + jnp.arange(-1, 2, dtype=jnp.int32)
        window_ok = (window_raw >= 0) & (window_raw < NB)
        window_ids = jnp.clip(window_raw, 0, NB - 1).astype(jnp.int32)
        picked = rand_ids[block_index]

        def collect(table):
            win_part = jnp.transpose(table[window_ids], (2, 3, 0, 1, 4))
            glob_part = jnp.transpose(table[glob_ids], (2, 3, 0, 1, 4))
            rand_part = jnp.transpose(table[picked, :, group_col], (0, 3, 1, 2, 4))
            joined = jnp.concatenate((win_part, glob_part, rand_part), axis=2)
            return joined.reshape(groups, GROUP_HEADS, key_span, HEAD_DIM).astype(jnp.float32)

        keys_all = collect(key_five)
        vals_all = collect(value_five)
        key_valid = jnp.concatenate((jnp.repeat(window_ok, BLOCK), jnp.ones(((GLOBALS + ROUNDS) * BLOCK,), jnp.bool_)))
        q_block = query_five[block_index].astype(jnp.float32)
        d_block = cot_five[block_index].astype(jnp.float32)
        scores = jnp.einsum('qghd,ghkd->ghqk', q_block, keys_all) * score_scale
        scores = jnp.where(key_valid, scores, NEG_FILL)
        row_max = jnp.max(scores, axis=-1, keepdims=True)
        weights = jnp.where(key_valid, jnp.exp(scores - row_max), 0.0)
        log_total = row_max + jnp.log(jnp.sum(weights, axis=-1, keepdims=True))
        probs = jnp.where(key_valid, jnp.exp(scores - log_total), 0.0)
        probs_b = probs.astype(jnp.bfloat16).astype(jnp.float32)
        attended = jnp.einsum('ghqk,ghkd->qghd', probs_b, vals_all).astype(jnp.bfloat16)
        row_dot = jnp.sum(d_block * attended.astype(jnp.float32), axis=-1)
        row_dot = jnp.transpose(row_dot, (1, 2, 0))[..., None]
        dprob = jnp.einsum('qghd,ghkd->ghqk', d_block, vals_all)
        dscore = (probs * (dprob - row_dot)).astype(jnp.bfloat16).astype(jnp.float32)
        grad_q = (jnp.einsum('ghqk,ghkd->qghd', dscore, keys_all) * score_scale).astype(jnp.bfloat16)
        term_k = jnp.einsum('ghqk,qghd->ghkd', dscore, q_block) * score_scale
        term_v = jnp.einsum('ghqk,qghd->ghkd', probs_b, d_block)

        def spread(total, term):
            term = term.reshape(groups, GROUP_HEADS, key_kinds, BLOCK, HEAD_DIM)
            win_term = jnp.transpose(term[:, :, 0:3], (2, 3, 0, 1, 4))
            glob_term = jnp.transpose(term[:, :, 3:3 + GLOBALS], (2, 3, 0, 1, 4))
            rand_term = jnp.transpose(term[:, :, 3 + GLOBALS:], (0, 2, 3, 1, 4))
            rand_term = lax.optimization_barrier(rand_term.astype(jnp.bfloat16)).astype(jnp.float32)
            total = total.at[window_ids].add(win_term)
            total = total.at[glob_ids].add(glob_term)
            total = total.at[picked, :, group_col].add(rand_term)
            return total

        return (spread(grad_k, term_k), spread(grad_v, term_v)), (attended, grad_q)

    zero_grad = jnp.zeros((NB, BLOCK, groups, GROUP_HEADS, HEAD_DIM), jnp.float32)
    grads, stacked = lax.scan(one_block, (zero_grad, zero_grad), jnp.arange(NB, dtype=jnp.int32))
    attended = stacked[0].reshape(NB * BLOCK, features)
    grad_query = stacked[1].reshape(NB * BLOCK, features)
    grad_key = grads[0].reshape(NB * BLOCK, features).astype(jnp.bfloat16)
    grad_value = grads[1].reshape(NB * BLOCK, features).astype(jnp.bfloat16)
    return attended, grad_query, grad_key, grad_value
```

```python
import functools
import math

import jax
import jax.numpy as jnp
from jax import lax
from jax.experimental import pallas as pl
from jax.experimental.pallas import tpu as pltpu
from jax.sharding import PartitionSpec as P

HEAD_DIM = 64
GROUP_HEADS = 8
BLOCK = 64
GLOBALS = 2
ROUNDS = 3
KINDS = 3 + GLOBALS + ROUNDS
SPAN = KINDS * BLOCK
NEG_FILL = -1e30
SCALE = HEAD_DIM ** -0.5
EXP_SCALE = SCALE * math.log2(math.e)
VMEM = pl.BlockSpec(memory_space=pltpu.VMEM)
SMEM = pl.BlockSpec(memory_space=pltpu.SMEM)


def head_of(ref, head):
    return ref[:, head * HEAD_DIM : (head + 1) * HEAD_DIM]


def pack_kernel(repeat, q_ref, k_ref, v_ref, c_ref, out_ref):
    for dst in range(out_ref.shape[0]):
        head = dst // repeat
        out_ref[dst, :, 0:128] = jnp.concatenate((head_of(k_ref, head), head_of(v_ref, head)), axis=1)
        out_ref[dst, :, 128:256] = jnp.concatenate((head_of(q_ref, head), head_of(c_ref, head)), axis=1)


def unpack_kernel(repeat, in_ref, att_ref, dq_ref, dk_ref, dv_ref):
    heads = in_ref.shape[0] // repeat
    for out_ref, col in ((dq_ref, 0), (att_ref, 64), (dk_ref, 128), (dv_ref, 192)):
        for pair in range(heads // 2):
            out_ref[:, pair * 128 : (pair + 1) * 128] = jnp.concatenate(
                [in_ref[(2 * pair + half) * repeat, :, col : col + 64] for half in range(2)], axis=1
            )


def attend_kernel(blocks_per_device, repeat, glob_ref, owner_ref, local_ref, in_ref, out_ref, acc_ref):
    blocks = in_ref.shape[0] // BLOCK
    group = lax.axis_index("ctx") // (repeat * GROUP_HEADS)
    acc_ref[...] = jnp.zeros_like(acc_ref)

    def step(i):
        ids = [jnp.maximum(i - 1, 0), i, jnp.minimum(i + 1, blocks - 1)]
        ids += [glob_ref[n] for n in range(GLOBALS)]
        for n in range(ROUNDS):
            col = group * ROUNDS + n
            ids.append(owner_ref[i, col] * blocks_per_device + local_ref[i, col])
        rows = [pl.ds(pl.multiple_of(one * BLOCK, BLOCK), BLOCK) for one in ids]
        kv = jnp.concatenate([in_ref[r, 0:128] for r in rows], axis=0)
        qc = in_ref[rows[1], 128:256]
        zero = jnp.zeros_like(qc)
        low = lax.broadcasted_iota(jnp.int32, qc.shape, 1) < HEAD_DIM
        q_part = jnp.where(low, qc, zero)
        c_part = jnp.where(low, zero, qc)
        both = lax.dot_general(
            jnp.concatenate((q_part, c_part), axis=0),
            kv,
            (((1,), (1,)), ((), ())),
            preferred_element_type=jnp.float32,
        )
        place = lax.broadcasted_iota(jnp.int32, (1, SPAN), 1)
        absent = ((place < BLOCK) & (i == 0)) | (
            (place >= 2 * BLOCK) & (place < 3 * BLOCK) & (i == blocks - 1)
        )
        scores = jnp.where(absent, NEG_FILL, both[:BLOCK])
        dprob = both[BLOCK:]
        row_max = jnp.max(scores, axis=-1, keepdims=True)
        weights = jnp.exp2((scores - row_max) * EXP_SCALE)
        probs = weights * (1.0 / jnp.sum(weights, axis=-1, keepdims=True))
        row_dot = jnp.sum(probs * dprob, axis=-1, keepdims=True)
        dscore = probs * (dprob - row_dot)
        pd = jnp.concatenate((probs.astype(jnp.bfloat16), dscore.astype(jnp.bfloat16)), axis=0)
        res = jnp.dot(pd, kv, preferred_element_type=jnp.float32)
        out_ref[rows[1], 0:128] = jnp.where(low, res[BLOCK:] * SCALE, res[:BLOCK]).astype(jnp.bfloat16)
        terms = lax.dot_general(
            pd,
            jnp.concatenate((c_part, q_part), axis=0),
            (((0,), (0,)), ((), ())),
            preferred_element_type=jnp.float32,
        )
        for n, r in enumerate(rows):
            acc_ref[r, :] += terms[n * BLOCK : (n + 1) * BLOCK]

    pl.loop(0, blocks)(step)

    def finish(i):
        r = pl.ds(pl.multiple_of(i * 256, 256), 256)
        acc = acc_ref[r, :]
        low = lax.broadcasted_iota(jnp.int32, acc.shape, 1) < HEAD_DIM
        out_ref[r, 128:256] = jnp.where(low, acc * SCALE, acc).astype(jnp.bfloat16)

    pl.loop(0, blocks * BLOCK // 256)(finish)


def per_device(query, key, value, cotangent, global_ids, rand_owner, rand_local):
    tokens, features = query.shape
    heads = features // HEAD_DIM
    devices = lax.axis_size("ctx")
    repeat = max(1, devices // heads)
    params = pltpu.CompilerParams(vmem_limit_bytes=48 << 20)
    packed = pl.pallas_call(
        functools.partial(pack_kernel, repeat),
        out_shape=jax.ShapeDtypeStruct((devices, tokens, 256), jnp.bfloat16),
        in_specs=[VMEM] * 4,
        out_specs=VMEM,
        compiler_params=params,
    )(query, key, value, cotangent)
    arrived = lax.all_to_all(packed, "ctx", 0, 0, tiled=True).reshape(devices * tokens, 256)
    grads = pl.pallas_call(
        functools.partial(attend_kernel, tokens // BLOCK, repeat),
        out_shape=jax.ShapeDtypeStruct((devices * tokens, 256), jnp.bfloat16),
        in_specs=[SMEM] * 3 + [VMEM],
        out_specs=VMEM,
        scratch_shapes=[pltpu.VMEM((devices * tokens, 128), jnp.float32)],
        compiler_params=params,
    )(global_ids, rand_owner, rand_local, arrived)
    back = lax.all_to_all(grads.reshape(devices, tokens, 256), "ctx", 0, 0, tiled=True)
    return pl.pallas_call(
        functools.partial(unpack_kernel, repeat),
        out_shape=[jax.ShapeDtypeStruct((tokens, features), jnp.bfloat16)] * 4,
        in_specs=[VMEM],
        out_specs=[VMEM] * 4,
        compiler_params=params,
    )(back)


def solution(mesh):
    split = P(("groups", "ctx"), None)
    return jax.shard_map(
        per_device,
        mesh=mesh,
        in_specs=(split, split, split, split, P("groups"), P("groups", None), P("groups", None)),
        out_specs=(split, split, split, split),
        check_vma=False,
    )
```

```python
import functools
import math

import jax
import jax.numpy as jnp
from jax import lax
from jax.experimental import pallas as pl
from jax.experimental.pallas import tpu as pltpu
from jax.sharding import PartitionSpec as P

HEAD_DIM = 64
GROUP_HEADS = 8
BLOCK = 64
GLOBALS = 2
ROUNDS = 3
KINDS = 3 + GLOBALS + ROUNDS
SPAN = KINDS * BLOCK
NEG_FILL = -1e30
UNROLL = 8
SCALE = HEAD_DIM ** -0.5
EXP_SCALE = SCALE * math.log2(math.e)
VMEM = pl.BlockSpec(memory_space=pltpu.VMEM)
SMEM = pl.BlockSpec(memory_space=pltpu.SMEM)


def head_of(ref, head):
    return ref[:, head * HEAD_DIM : (head + 1) * HEAD_DIM]


def pack_kernel(repeat, q_ref, k_ref, v_ref, c_ref, out_ref):
    for dst in range(out_ref.shape[0]):
        head = dst // repeat
        out_ref[dst, :, 0:128] = jnp.concatenate((head_of(k_ref, head), head_of(v_ref, head)), axis=1)
        out_ref[dst, :, 128:256] = jnp.concatenate((head_of(q_ref, head), head_of(c_ref, head)), axis=1)


def unpack_kernel(repeat, in_ref, att_ref, dq_ref, dk_ref, dv_ref):
    heads = in_ref.shape[0] // repeat
    for out_ref, col in ((dq_ref, 0), (att_ref, 64), (dk_ref, 128), (dv_ref, 192)):
        for pair in range(heads // 2):
            out_ref[:, pair * 128 : (pair + 1) * 128] = jnp.concatenate(
                [in_ref[(2 * pair + half) * repeat, :, col : col + 64] for half in range(2)], axis=1
            )


def attend_kernel(blocks_per_device, repeat, glob_ref, owner_ref, local_ref, in_ref, out_ref, acc_ref):
    blocks = in_ref.shape[0] // BLOCK
    group = lax.axis_index("ctx") // (repeat * GROUP_HEADS)
    acc_ref[...] = jnp.zeros_like(acc_ref)

    low = lax.broadcasted_iota(jnp.int32, (BLOCK, 128), 1) < HEAD_DIM
    place = lax.broadcasted_iota(jnp.int32, (1, SPAN), 1)

    def load(i):
        ids = [jnp.maximum(i - 1, 0), i, jnp.minimum(i + 1, blocks - 1)]
        ids += [glob_ref[n] for n in range(GLOBALS)]
        for n in range(ROUNDS):
            col = group * ROUNDS + n
            ids.append(owner_ref[i, col] * blocks_per_device + local_ref[i, col])
        rows = [pl.ds(pl.multiple_of(one * BLOCK, BLOCK), BLOCK) for one in ids]
        kv = jnp.concatenate([in_ref[r, 0:128] for r in rows], axis=0)
        qc = in_ref[rows[1], 128:256]
        zero = jnp.zeros_like(qc)
        return rows, kv, jnp.where(low, qc, zero), jnp.where(low, zero, qc)

    def products(kv, q_part, c_part):
        return lax.dot_general(
            jnp.concatenate((q_part, c_part), axis=0),
            kv,
            (((1,), (1,)), ((), ())),
            preferred_element_type=jnp.float32,
        )

    def softmax(i, both):
        absent = ((place < BLOCK) & (i == 0)) | (
            (place >= 2 * BLOCK) & (place < 3 * BLOCK) & (i == blocks - 1)
        )
        scores = jnp.where(absent, NEG_FILL, both[:BLOCK])
        dprob = both[BLOCK:]
        row_max = jnp.max(scores, axis=-1, keepdims=True)
        weights = jnp.exp2((scores - row_max) * EXP_SCALE)
        inverse = 1.0 / jnp.sum(weights, axis=-1, keepdims=True)
        row_dot = jnp.sum(weights * dprob, axis=-1, keepdims=True) * inverse
        probs = weights * inverse
        dscore = probs * (dprob - row_dot)
        return jnp.concatenate((probs.astype(jnp.bfloat16), dscore.astype(jnp.bfloat16)), axis=0)

    def query_side(row, kv, pd):
        res = jnp.dot(pd, kv, preferred_element_type=jnp.float32)
        out_ref[row, 0:128] = jnp.where(low, res[BLOCK:] * SCALE, res[:BLOCK]).astype(jnp.bfloat16)

    def key_side(q_part, c_part, pd):
        return lax.dot_general(
            pd,
            jnp.concatenate((c_part, q_part), axis=0),
            (((0,), (0,)), ((), ())),
            preferred_element_type=jnp.float32,
        )

    def step(j):
        mine = [j * UNROLL + u for u in range(UNROLL)]
        loaded = [load(i) for i in mine]
        both = [products(*one[1:]) for one in loaded]
        pds = [softmax(i, one) for i, one in zip(mine, both)]
        terms = []
        for (rows, kv, q_part, c_part), pd in zip(loaded, pds):
            query_side(rows[1], kv, pd)
            terms.append(key_side(q_part, c_part, pd))
        for one, term in zip(loaded, terms):
            for n, r in enumerate(one[0]):
                acc_ref[r, :] += term[n * BLOCK : (n + 1) * BLOCK]

    pl.loop(0, blocks // UNROLL)(step)

    def finish(i):
        r = pl.ds(pl.multiple_of(i * 256, 256), 256)
        acc = acc_ref[r, :]
        left = lax.broadcasted_iota(jnp.int32, acc.shape, 1) < HEAD_DIM
        out_ref[r, 128:256] = jnp.where(left, acc * SCALE, acc).astype(jnp.bfloat16)

    pl.loop(0, blocks * BLOCK // 256)(finish)


def per_device(query, key, value, cotangent, global_ids, rand_owner, rand_local):
    tokens, features = query.shape
    heads = features // HEAD_DIM
    devices = lax.axis_size("ctx")
    repeat = max(1, devices // heads)
    params = pltpu.CompilerParams(vmem_limit_bytes=48 << 20)
    packed = pl.pallas_call(
        functools.partial(pack_kernel, repeat),
        out_shape=jax.ShapeDtypeStruct((devices, tokens, 256), jnp.bfloat16),
        in_specs=[VMEM] * 4,
        out_specs=VMEM,
        compiler_params=params,
    )(query, key, value, cotangent)
    arrived = lax.all_to_all(packed, "ctx", 0, 0, tiled=True).reshape(devices * tokens, 256)
    grads = pl.pallas_call(
        functools.partial(attend_kernel, tokens // BLOCK, repeat),
        out_shape=jax.ShapeDtypeStruct((devices * tokens, 256), jnp.bfloat16),
        in_specs=[SMEM] * 3 + [VMEM],
        out_specs=VMEM,
        scratch_shapes=[pltpu.VMEM((devices * tokens, 128), jnp.float32)],
        compiler_params=params,
    )(global_ids, rand_owner, rand_local, arrived)
    back = lax.all_to_all(grads.reshape(devices, tokens, 256), "ctx", 0, 0, tiled=True)
    return pl.pallas_call(
        functools.partial(unpack_kernel, repeat),
        out_shape=[jax.ShapeDtypeStruct((tokens, features), jnp.bfloat16)] * 4,
        in_specs=[VMEM],
        out_specs=[VMEM] * 4,
        compiler_params=params,
    )(back)


def solution(mesh):
    split = P(("groups", "ctx"), None)
    return jax.shard_map(
        per_device,
        mesh=mesh,
        in_specs=(split, split, split, split, P("groups"), P("groups", None), P("groups", None)),
        out_specs=(split, split, split, split),
        check_vma=False,
    )
```

```python
import functools
import math

import jax
import jax.numpy as jnp
from jax import lax
from jax.experimental import pallas as pl
from jax.experimental.pallas import tpu as pltpu
from jax.sharding import PartitionSpec as P

HEAD_DIM = 64
GROUP_HEADS = 8
BLOCK = 64
GLOBALS = 2
ROUNDS = 3
KINDS = 3 + GLOBALS + ROUNDS
SPAN = KINDS * BLOCK
PAIR = 2 * HEAD_DIM
NEG_FILL = -1e30
UNROLL = 8
CHUNKS = 4
SCALE = HEAD_DIM ** -0.5
EXP_SCALE = SCALE * math.log2(math.e)
VMEM = pl.BlockSpec(memory_space=pltpu.VMEM)
SMEM = pl.BlockSpec(memory_space=pltpu.SMEM)
HBM = pl.BlockSpec(memory_space=pltpu.HBM)


def pack_kernel(repeat, q_ref, k_ref, v_ref, c_ref, out_ref, buf_ref, tile_ref, sems, out_sems):
    tokens, features = q_ref.shape
    size = tokens // CHUNKS
    copies = []
    for t in range(CHUNKS):
        rows = pl.ds(t * size, size)
        copies.append(
            [
                pltpu.make_async_copy(ref.at[rows], buf_ref.at[n, rows], sems.at[n, t])
                for n, ref in enumerate((k_ref, v_ref, q_ref, c_ref))
            ]
        )
    for one in copies:
        for copy in one:
            copy.start()
    sent = []
    for t in range(CHUNKS):
        for copy in copies[t]:
            copy.wait()
        rows = pl.ds(t * size, size)
        for half in range(2):
            place = pl.ds(half * tokens + t * size, size)
            for pair in range(features // PAIR):
                cols = pl.ds(pair * PAIR, PAIR)
                first = buf_ref[2 * half, rows, cols]
                second = buf_ref[2 * half + 1, rows, cols]
                even = jnp.concatenate((first[:, :HEAD_DIM], second[:, :HEAD_DIM]), axis=1)
                odd = jnp.concatenate((first[:, HEAD_DIM:], second[:, HEAD_DIM:]), axis=1)
                for n in range(repeat):
                    tile_ref[2 * pair * repeat + n, place, :] = even
                    tile_ref[(2 * pair + 1) * repeat + n, place, :] = odd
            sent.append(
                pltpu.make_async_copy(tile_ref.at[:, place], out_ref.at[:, place], out_sems.at[half, t])
            )
            sent[-1].start()
    for copy in sent:
        copy.wait()


def unpack_kernel(repeat, in_ref, att_ref, dq_ref, dk_ref, dv_ref, buf_ref, sems):
    tokens, features = att_ref.shape
    size = tokens // CHUNKS
    copies = []
    for t in range(CHUNKS):
        rows = pl.ds(t * size, size)
        for half in range(2):
            place = pl.ds(half * tokens + t * size, size)
            for pair in range(features // PAIR):
                cols = pl.ds(pair * PAIR, PAIR)
                even = in_ref[2 * pair * repeat, place, :]
                odd = in_ref[(2 * pair + 1) * repeat, place, :]
                buf_ref[2 * half, rows, cols] = jnp.concatenate(
                    (even[:, :HEAD_DIM], odd[:, :HEAD_DIM]), axis=1
                )
                buf_ref[2 * half + 1, rows, cols] = jnp.concatenate(
                    (even[:, HEAD_DIM:], odd[:, HEAD_DIM:]), axis=1
                )
        for n, ref in enumerate((dq_ref, att_ref, dk_ref, dv_ref)):
            copies.append(pltpu.make_async_copy(buf_ref.at[n, rows], ref.at[rows], sems.at[n, t]))
            copies[-1].start()
    for copy in copies:
        copy.wait()


def attend_kernel(tokens, repeat, glob_ref, owner_ref, local_ref, in_ref, out_ref, acc_ref):
    per_device = tokens // BLOCK
    blocks = in_ref.shape[0] // (2 * BLOCK)
    group = lax.axis_index("ctx") // (repeat * GROUP_HEADS)
    acc_ref[...] = jnp.zeros_like(acc_ref)
    low = lax.broadcasted_iota(jnp.int32, (BLOCK, PAIR), 1) < HEAD_DIM
    place = lax.broadcasted_iota(jnp.int32, (1, SPAN), 1)

    def rows_at(owner, local):
        start = owner * (2 * tokens) + local * BLOCK
        return pl.ds(pl.multiple_of(start, BLOCK), BLOCK)

    def rows_of(i):
        return rows_at(lax.div(i, per_device), lax.rem(i, per_device))

    def load(i):
        rows = [rows_of(one) for one in (jnp.maximum(i - 1, 0), i, jnp.minimum(i + 1, blocks - 1))]
        rows += [rows_of(glob_ref[n]) for n in range(GLOBALS)]
        for n in range(ROUNDS):
            entry = group * ROUNDS + n
            rows.append(rows_at(owner_ref[entry, i], local_ref[entry, i]))
        kv = jnp.concatenate([in_ref[r, :] for r in rows], axis=0)
        mine = pl.ds(pl.multiple_of(rows[1].start + tokens, BLOCK), BLOCK)
        qc = in_ref[mine, :]
        zero = jnp.zeros_like(qc)
        return rows, kv, jnp.where(low, qc, zero), jnp.where(low, zero, qc)

    def products(kv, q_part, c_part):
        return lax.dot_general(
            jnp.concatenate((q_part, c_part), axis=0),
            kv,
            (((1,), (1,)), ((), ())),
            preferred_element_type=jnp.float32,
        )

    def softmax(i, both):
        absent = ((place < BLOCK) & (i == 0)) | (
            (place >= 2 * BLOCK) & (place < 3 * BLOCK) & (i == blocks - 1)
        )
        scores = jnp.where(absent, NEG_FILL, both[:BLOCK])
        dprob = both[BLOCK:]
        row_max = jnp.max(scores, axis=-1, keepdims=True)
        weights = jnp.exp2((scores - row_max) * EXP_SCALE)
        inverse = 1.0 / jnp.sum(weights, axis=-1, keepdims=True)
        row_dot = jnp.sum(weights * dprob, axis=-1, keepdims=True) * inverse
        probs = weights * inverse
        dscore = probs * (dprob - row_dot)
        return jnp.concatenate((probs.astype(jnp.bfloat16), dscore.astype(jnp.bfloat16)), axis=0)

    def query_side(row, kv, pd):
        res = jnp.dot(pd, kv, preferred_element_type=jnp.float32)
        out_ref[row, :] = jnp.where(low, res[BLOCK:] * SCALE, res[:BLOCK]).astype(jnp.bfloat16)

    def key_side(q_part, c_part, pd):
        return lax.dot_general(
            pd,
            jnp.concatenate((c_part, q_part), axis=0),
            (((0,), (0,)), ((), ())),
            preferred_element_type=jnp.float32,
        )

    def step(j):
        mine = [j * UNROLL + u for u in range(UNROLL)]
        loaded = [load(i) for i in mine]
        both = [products(*one[1:]) for one in loaded]
        pds = [softmax(i, one) for i, one in zip(mine, both)]
        terms = []
        for (rows, kv, q_part, c_part), pd in zip(loaded, pds):
            query_side(rows[1], kv, pd)
            terms.append(key_side(q_part, c_part, pd))
        for one, term in zip(loaded, terms):
            for n, r in enumerate(one[0]):
                acc_ref[r, :] += term[n * BLOCK : (n + 1) * BLOCK]

    pl.loop(0, blocks // UNROLL)(step)

    def finish(d):
        start = pl.multiple_of(d * (2 * tokens), tokens)
        acc = acc_ref[pl.ds(start, tokens), :]
        left = lax.broadcasted_iota(jnp.int32, acc.shape, 1) < HEAD_DIM
        result = jnp.where(left, acc * SCALE, acc).astype(jnp.bfloat16)
        out_ref[pl.ds(pl.multiple_of(start + tokens, tokens), tokens), :] = result

    pl.loop(0, blocks // per_device)(finish)


def per_device(query, key, value, cotangent, global_ids, rand_owner, rand_local):
    tokens, features = query.shape
    heads = features // HEAD_DIM
    devices = lax.axis_size("ctx")
    repeat = max(1, devices // heads)
    params = pltpu.CompilerParams(vmem_limit_bytes=48 << 20)
    scratch = [
        pltpu.VMEM((4, tokens, features), jnp.bfloat16),
        pltpu.SemaphoreType.DMA((4, CHUNKS)),
    ]
    packed = pl.pallas_call(
        functools.partial(pack_kernel, repeat),
        out_shape=jax.ShapeDtypeStruct((devices, 2 * tokens, PAIR), jnp.bfloat16),
        in_specs=[HBM] * 4,
        out_specs=HBM,
        scratch_shapes=[
            scratch[0],
            pltpu.VMEM((devices, 2 * tokens, PAIR), jnp.bfloat16),
            scratch[1],
            pltpu.SemaphoreType.DMA((2, CHUNKS)),
        ],
        compiler_params=pltpu.CompilerParams(vmem_limit_bytes=60 << 20),
    )(query, key, value, cotangent)
    arrived = lax.all_to_all(packed, "ctx", 0, 0, tiled=True)
    grads = pl.pallas_call(
        functools.partial(attend_kernel, tokens, repeat),
        out_shape=jax.ShapeDtypeStruct((devices * 2 * tokens, PAIR), jnp.bfloat16),
        in_specs=[SMEM] * 3 + [VMEM],
        out_specs=VMEM,
        scratch_shapes=[pltpu.VMEM((devices * 2 * tokens, PAIR), jnp.float32)],
        compiler_params=params,
    )(global_ids, rand_owner.T, rand_local.T, arrived.reshape(devices * 2 * tokens, PAIR))
    back = lax.all_to_all(grads.reshape(devices, 2 * tokens, PAIR), "ctx", 0, 0, tiled=True)
    return pl.pallas_call(
        functools.partial(unpack_kernel, repeat),
        out_shape=[jax.ShapeDtypeStruct((tokens, features), jnp.bfloat16)] * 4,
        in_specs=[VMEM],
        out_specs=[HBM] * 4,
        scratch_shapes=scratch,
        compiler_params=params,
    )(back)


def solution(mesh):
    split = P(("groups", "ctx"), None)
    return jax.shard_map(
        per_device,
        mesh=mesh,
        in_specs=(split, split, split, split, P("groups"), P("groups", None), P("groups", None)),
        out_specs=(split, split, split, split),
        check_vma=False,
    )
```

```python
import functools
import math

import jax
import jax.numpy as jnp
from jax import lax
from jax.experimental import pallas as pl
from jax.experimental.pallas import tpu as pltpu
from jax.sharding import PartitionSpec as P

HEAD_DIM = 64
GROUP_HEADS = 8
BLOCK = 64
GLOBALS = 2
ROUNDS = 3
KINDS = 3 + GLOBALS + ROUNDS
SPAN = KINDS * BLOCK
PAIR = 2 * HEAD_DIM
NEG_FILL = -1e30
UNROLL = 8
CHUNKS = 4
TOGETHER = 2
SCALE = HEAD_DIM ** -0.5
EXP_SCALE = SCALE * math.log2(math.e)
VMEM = pl.BlockSpec(memory_space=pltpu.VMEM)
SMEM = pl.BlockSpec(memory_space=pltpu.SMEM)
HBM = pl.BlockSpec(memory_space=pltpu.HBM)


def halves(first, second):
    even = jnp.concatenate((first[:, :HEAD_DIM], second[:, :HEAD_DIM]), axis=1)
    odd = jnp.concatenate((first[:, HEAD_DIM:], second[:, HEAD_DIM:]), axis=1)
    return even, odd


def fill_tiles(first_ref, second_ref, tile_ref, place, repeat):
    for pair in range(first_ref.shape[-1] // PAIR):
        cols = pl.ds(pair * PAIR, PAIR)
        even, odd = halves(first_ref[:, cols], second_ref[:, cols])
        for n in range(repeat):
            tile_ref[2 * pair * repeat + n, place, :] = even
            tile_ref[(2 * pair + 1) * repeat + n, place, :] = odd


def send_far(tile_ref, far_refs, sems):
    count = len(far_refs)
    mine = lax.rem(lax.axis_index("ctx"), count)
    copies = []
    for m, ref in enumerate(far_refs):
        copies.append(pltpu.make_async_copy(tile_ref.at[mine ^ m], ref, sems.at[m]))
        copies[-1].start()
    return copies


def sides(refs, count):
    width = refs[0].shape[1] // 2
    upper = lax.div(lax.axis_index("ctx"), count)
    near = pl.ds(pl.multiple_of(upper * width, PAIR), width)
    far = pl.ds(pl.multiple_of((1 - upper) * width, PAIR), width)
    return near, far


def pack_keys_kernel(repeat, k_ref, v_ref, out_ref, buf_ref, tile_ref, sems, out_sems):
    size = k_ref.shape[0] // CHUNKS
    places = [pl.ds(t * size, size) for t in range(CHUNKS)]
    copies = []
    for t, rows in enumerate(places):
        for n, ref in enumerate((k_ref, v_ref)):
            copies.append(pltpu.make_async_copy(ref.at[rows], buf_ref.at[n, rows], sems.at[n, t]))
            copies[-1].start()
    sent = []
    for t, rows in enumerate(places):
        copies[2 * t].wait()
        copies[2 * t + 1].wait()
        fill_tiles(buf_ref.at[0, rows], buf_ref.at[1, rows], tile_ref, rows, repeat)
        sent.append(pltpu.make_async_copy(tile_ref.at[:, rows], out_ref.at[:, rows], out_sems.at[t]))
        sent[-1].start()
    for copy in sent:
        copy.wait()


def pack_queries_kernel(repeat, count, far, waits, q_ref, c_ref, *rest):
    rest = rest[waits:]
    out_refs, (buf_ref, tile_ref, sems, out_sems) = rest[:count], rest[count:]
    cols = sides((q_ref,), count)[far]
    copies = []
    for n, ref in enumerate((q_ref, c_ref)):
        copies.append(pltpu.make_async_copy(ref.at[:, cols], buf_ref.at[n], sems.at[n]))
        copies[-1].start()
    for copy in copies:
        copy.wait()
    fill_tiles(buf_ref.at[0], buf_ref.at[1], tile_ref, pl.ds(0, q_ref.shape[0]), repeat)
    for copy in send_far(tile_ref, out_refs, out_sems):
        copy.wait()


def unpack_kernel(repeat, in_ref, att_ref, dq_ref, dk_ref, dv_ref, buf_ref, sems):
    tokens, features = att_ref.shape
    size = tokens // CHUNKS
    copies = []
    for t in range(CHUNKS):
        rows = pl.ds(t * size, size)
        for half in range(2):
            place = pl.ds(half * tokens + t * size, size)
            for pair in range(features // PAIR):
                cols = pl.ds(pair * PAIR, PAIR)
                even = in_ref[2 * pair * repeat, place, :]
                odd = in_ref[(2 * pair + 1) * repeat, place, :]
                buf_ref[2 * half, rows, cols] = jnp.concatenate(
                    (even[:, :HEAD_DIM], odd[:, :HEAD_DIM]), axis=1
                )
                buf_ref[2 * half + 1, rows, cols] = jnp.concatenate(
                    (even[:, HEAD_DIM:], odd[:, HEAD_DIM:]), axis=1
                )
        for n, ref in enumerate((dq_ref, att_ref, dk_ref, dv_ref)):
            copies.append(pltpu.make_async_copy(buf_ref.at[n, rows], ref.at[rows], sems.at[n, t]))
            copies[-1].start()
    for copy in copies:
        copy.wait()


def attend(tables, kv_ref, acc_ref, blocks, group, items):
    glob_ref, owner_ref, local_ref = tables
    per_device = kv_ref.shape[0] // BLOCK // lax.axis_size("ctx")
    low = lax.broadcasted_iota(jnp.int32, (BLOCK, PAIR), 1) < HEAD_DIM
    place = lax.broadcasted_iota(jnp.int32, (1, SPAN), 1)

    def load(i, qc):
        ids = [jnp.maximum(i - 1, 0), i, jnp.minimum(i + 1, blocks - 1)]
        ids += [glob_ref[n] for n in range(GLOBALS)]
        for n in range(ROUNDS):
            entry = group * ROUNDS + n
            ids.append(owner_ref[entry, i] * per_device + local_ref[entry, i])
        rows = [pl.ds(pl.multiple_of(one * BLOCK, BLOCK), BLOCK) for one in ids]
        kv = jnp.concatenate([kv_ref[r, :] for r in rows], axis=0)
        zero = jnp.zeros_like(qc)
        return rows, kv, jnp.where(low, qc, zero), jnp.where(low, zero, qc)

    def products(kv, q_part, c_part):
        return lax.dot_general(
            jnp.concatenate((q_part, c_part), axis=0),
            kv,
            (((1,), (1,)), ((), ())),
            preferred_element_type=jnp.float32,
        )

    def softmax(i, both):
        absent = ((place < BLOCK) & (i == 0)) | (
            (place >= 2 * BLOCK) & (place < 3 * BLOCK) & (i == blocks - 1)
        )
        scores = jnp.where(absent, NEG_FILL, both[:BLOCK])
        dprob = both[BLOCK:]
        row_max = jnp.max(scores, axis=-1, keepdims=True)
        weights = jnp.exp2((scores - row_max) * EXP_SCALE)
        inverse = 1.0 / jnp.sum(weights, axis=-1, keepdims=True)
        row_dot = jnp.sum(weights * dprob, axis=-1, keepdims=True) * inverse
        probs = weights * inverse
        dscore = probs * (dprob - row_dot)
        return jnp.concatenate((probs.astype(jnp.bfloat16), dscore.astype(jnp.bfloat16)), axis=0)

    def query_side(kv, pd):
        res = jnp.dot(pd, kv, preferred_element_type=jnp.float32)
        return jnp.where(low, res[BLOCK:] * SCALE, res[:BLOCK]).astype(jnp.bfloat16)

    def key_side(q_part, c_part, pd):
        return lax.dot_general(
            pd,
            jnp.concatenate((c_part, q_part), axis=0),
            (((0,), (0,)), ((), ())),
            preferred_element_type=jnp.float32,
        )

    loaded = [load(i, qc) for i, qc, _ in items]
    both = [products(*one[1:]) for one in loaded]
    pds = [softmax(item[0], one) for item, one in zip(items, both)]
    terms = []
    for (_, kv, q_part, c_part), pd, item in zip(loaded, pds, items):
        item[2](query_side(kv, pd))
        terms.append(key_side(q_part, c_part, pd))
    for one, term in zip(loaded, terms):
        for n, r in enumerate(one[0]):
            acc_ref[r, :] += term[n * BLOCK : (n + 1) * BLOCK]


def my_group(repeat):
    return lax.axis_index("ctx") // (repeat * GROUP_HEADS)


def near_kernel(repeat, count, glob_ref, owner_ref, local_ref, kv_ref, *rest):
    qc_refs, (acc_ref, out_ref, near_ref) = rest[:count], rest[count:]
    tokens = qc_refs[0].shape[0]
    mine = lax.rem(lax.axis_index("ctx"), count)
    base = lax.axis_index("ctx") - mine
    blocks = kv_ref.shape[0] // BLOCK
    per_device = tokens // BLOCK
    acc_ref[...] = jnp.zeros_like(acc_ref)
    for m, ref in enumerate(qc_refs):
        near_ref[mine ^ m] = ref[...]

    def step(j):
        items = []
        for u in range(UNROLL):
            place = j * UNROLL + u
            device, local = lax.div(place, per_device), lax.rem(place, per_device)
            rows = pl.ds(pl.multiple_of(local * BLOCK, BLOCK), BLOCK)

            def put(value, device=device, rows=rows):
                out_ref[device, rows, :] = value

            items.append((base * per_device + place, near_ref[device, rows, :], put))
        attend((glob_ref, owner_ref, local_ref), kv_ref, acc_ref, blocks, my_group(repeat), items)

    pl.loop(0, count * per_device // UNROLL)(step)


def far_step(repeat, count, first, tables, kv_ref, qc_refs, acc_ref, out_refs):
    me = lax.axis_index("ctx")
    mine = lax.rem(me, count)
    base = me - mine
    items = []
    for m, (qc_ref, out_ref) in enumerate(zip(qc_refs, out_refs)):
        source = (count - base) + (mine ^ (first + m))
        per_device = qc_ref.shape[0] // BLOCK
        for local in range(per_device):
            rows = pl.ds(local * BLOCK, BLOCK)

            def put(value, out_ref=out_ref, rows=rows):
                out_ref[rows, :] = value

            items.append((source * per_device + local, qc_ref[rows, :], put))
    attend(tables, kv_ref, acc_ref, kv_ref.shape[0] // BLOCK, my_group(repeat), items)


def far_kernel(repeat, count, first, glob_ref, owner_ref, local_ref, kv_ref, acc_in_ref, *rest):
    qc_refs, acc_ref, out_refs = rest[:TOGETHER], rest[TOGETHER], rest[TOGETHER + 1 :]
    acc_ref[...] = acc_in_ref[...]
    far_step(repeat, count, first, (glob_ref, owner_ref, local_ref), kv_ref, qc_refs, acc_ref, out_refs)


def last_kernel(repeat, count, first, glob_ref, owner_ref, local_ref, kv_ref, acc_in_ref, *rest):
    qc_refs, near_ref, done_refs = rest[:TOGETHER], rest[TOGETHER], rest[TOGETHER + 1 : -3]
    out_ref, acc_ref, late_ref = rest[-3:]
    tokens = qc_refs[0].shape[0]
    me = lax.axis_index("ctx")
    mine = lax.rem(me, count)
    base = me - mine
    acc_ref[...] = acc_in_ref[...]
    late = [late_ref.at[m] for m in range(TOGETHER)]
    far_step(repeat, count, first, (glob_ref, owner_ref, local_ref), kv_ref, qc_refs, acc_ref, late)
    for j in range(count):
        out_ref[base + j, :tokens, :] = near_ref[j]
    for m, ref in enumerate(list(done_refs) + late):
        out_ref[(count - base) + (mine ^ m), :tokens, :] = ref[...]

    def finish(d):
        acc = acc_ref[pl.ds(pl.multiple_of(d * tokens, tokens), tokens), :]
        left = lax.broadcasted_iota(jnp.int32, acc.shape, 1) < HEAD_DIM
        out_ref[d, tokens:, :] = jnp.where(left, acc * SCALE, acc).astype(jnp.bfloat16)

    pl.loop(0, 2 * count)(finish)


def per_device(query, key, value, cotangent, global_ids, rand_owner, rand_local):
    tokens, features = query.shape
    heads = features // HEAD_DIM
    devices = lax.axis_size("ctx")
    repeat = max(1, devices // heads)
    count = devices // 2
    params = pltpu.CompilerParams(vmem_limit_bytes=48 << 20)
    roomy = pltpu.CompilerParams(vmem_limit_bytes=60 << 20)
    tile = jax.ShapeDtypeStruct((tokens, PAIR), jnp.bfloat16)

    packed = pl.pallas_call(
        functools.partial(pack_keys_kernel, repeat),
        out_shape=jax.ShapeDtypeStruct((devices, tokens, PAIR), jnp.bfloat16),
        in_specs=[HBM] * 2,
        out_specs=HBM,
        scratch_shapes=[
            pltpu.VMEM((2, tokens, features), jnp.bfloat16),
            pltpu.VMEM((devices, tokens, PAIR), jnp.bfloat16),
            pltpu.SemaphoreType.DMA((2, CHUNKS)),
            pltpu.SemaphoreType.DMA((CHUNKS,)),
        ],
        compiler_params=roomy,
    )(key, value)
    keys = lax.all_to_all(packed, "ctx", 0, 0, tiled=True).reshape(devices * tokens, PAIR)

    def swap(array, mask):
        return lax.ppermute(array, "ctx", [(i, i ^ mask) for i in range(devices)])

    def pack_queries(far, waits):
        return pl.pallas_call(
            functools.partial(pack_queries_kernel, repeat, count, far, len(waits)),
            out_shape=[tile] * count,
            in_specs=[HBM] * 2 + [pl.BlockSpec(memory_space=pl.ANY)] * len(waits),
            out_specs=[HBM] * count,
            scratch_shapes=[
                pltpu.VMEM((2, tokens, features // 2), jnp.bfloat16),
                pltpu.VMEM((count, tokens, PAIR), jnp.bfloat16),
                pltpu.SemaphoreType.DMA((2,)),
                pltpu.SemaphoreType.DMA((count,)),
            ],
            compiler_params=pltpu.CompilerParams(vmem_limit_bytes=16 << 20),
        )(query, cotangent, *waits)

    near_qc = pack_queries(0, [])
    near_qc = [one if m == 0 else swap(one, m) for m, one in enumerate(near_qc)]
    far_qc = pack_queries(1, [])
    far_qc = [swap(one, count + m) for m, one in enumerate(far_qc)]

    tables = (global_ids, rand_owner.T, rand_local.T)
    total = jax.ShapeDtypeStruct((devices * tokens, PAIR), jnp.float32)
    acc, near_out = pl.pallas_call(
        functools.partial(near_kernel, repeat, count),
        out_shape=[total, jax.ShapeDtypeStruct((count, tokens, PAIR), jnp.bfloat16)],
        in_specs=[SMEM] * 3 + [VMEM] * (1 + count),
        out_specs=[VMEM] * 2,
        scratch_shapes=[pltpu.VMEM((count, tokens, PAIR), jnp.bfloat16)],
        compiler_params=params,
        cost_estimate=pl.CostEstimate(flops=7 * 10**9, bytes_accessed=4 << 20, transcendentals=0),
    )(*tables, keys, *near_qc)
    done = []
    for first in range(0, count - TOGETHER, TOGETHER):
        acc, *outs = pl.pallas_call(
            functools.partial(far_kernel, repeat, count, first),
            out_shape=[total] + [tile] * TOGETHER,
            in_specs=[SMEM] * 3 + [VMEM] * (2 + TOGETHER),
            out_specs=[VMEM] * (1 + TOGETHER),
            compiler_params=params,
            cost_estimate=pl.CostEstimate(flops=2 * 10**9, bytes_accessed=4 << 20, transcendentals=0),
        )(*tables, keys, acc, *far_qc[first : first + TOGETHER])
        done += outs
    first = count - TOGETHER
    grads = pl.pallas_call(
        functools.partial(last_kernel, repeat, count, first),
        out_shape=jax.ShapeDtypeStruct((devices, 2 * tokens, PAIR), jnp.bfloat16),
        in_specs=[SMEM] * 3 + [VMEM] * (3 + count),
        out_specs=VMEM,
        scratch_shapes=[
            pltpu.VMEM((devices * tokens, PAIR), jnp.float32),
            pltpu.VMEM((TOGETHER, tokens, PAIR), jnp.bfloat16),
        ],
        compiler_params=params,
    )(*tables, keys, acc, *far_qc[first:], near_out, *done)
    back = lax.all_to_all(grads, "ctx", 0, 0, tiled=True)
    return pl.pallas_call(
        functools.partial(unpack_kernel, repeat),
        out_shape=[jax.ShapeDtypeStruct((tokens, features), jnp.bfloat16)] * 4,
        in_specs=[VMEM],
        out_specs=[HBM] * 4,
        scratch_shapes=[
            pltpu.VMEM((4, tokens, features), jnp.bfloat16),
            pltpu.SemaphoreType.DMA((4, CHUNKS)),
        ],
        compiler_params=params,
    )(back)


def solution(mesh):
    split = P(("groups", "ctx"), None)
    return jax.shard_map(
        per_device,
        mesh=mesh,
        in_specs=(split, split, split, split, P("groups"), P("groups", None), P("groups", None)),
        out_specs=(split, split, split, split),
        check_vma=False,
    )
```

```python
import functools
import math

import jax
import jax.numpy as jnp
from jax import lax
from jax.experimental import pallas as pl
from jax.experimental.pallas import tpu as pltpu
from jax.sharding import PartitionSpec as P

HEAD_DIM = 64
GROUP_HEADS = 8
BLOCK = 64
GLOBALS = 2
ROUNDS = 3
KINDS = 3 + GLOBALS + ROUNDS
SPAN = KINDS * BLOCK
PAIR = 2 * HEAD_DIM
NEG_FILL = -1e30
UNROLL = 8
CHUNKS = 4
PARTS = (4, 2, 2)
SCALE = HEAD_DIM ** -0.5
EXP_SCALE = SCALE * math.log2(math.e)
VMEM = pl.BlockSpec(memory_space=pltpu.VMEM)
SMEM = pl.BlockSpec(memory_space=pltpu.SMEM)
HBM = pl.BlockSpec(memory_space=pltpu.HBM)


def halves(first, second):
    even = jnp.concatenate((first[:, :HEAD_DIM], second[:, :HEAD_DIM]), axis=1)
    odd = jnp.concatenate((first[:, HEAD_DIM:], second[:, HEAD_DIM:]), axis=1)
    return even, odd


def fill_tiles(first_ref, second_ref, tile_ref, place, repeat):
    for pair in range(first_ref.shape[-1] // PAIR):
        cols = pl.ds(pair * PAIR, PAIR)
        even, odd = halves(first_ref[:, cols], second_ref[:, cols])
        for n in range(repeat):
            tile_ref[2 * pair * repeat + n, place, :] = even
            tile_ref[(2 * pair + 1) * repeat + n, place, :] = odd


def send_far(tile_ref, far_refs, sems):
    count = len(far_refs)
    mine = lax.rem(lax.axis_index("ctx"), count)
    copies = []
    for m, ref in enumerate(far_refs):
        copies.append(pltpu.make_async_copy(tile_ref.at[mine ^ m], ref, sems.at[m]))
        copies[-1].start()
    return copies


def sides(refs, count):
    width = refs[0].shape[1] // 2
    upper = lax.div(lax.axis_index("ctx"), count)
    near = pl.ds(pl.multiple_of(upper * width, PAIR), width)
    far = pl.ds(pl.multiple_of((1 - upper) * width, PAIR), width)
    return near, far


def pack_keys_kernel(repeat, k_ref, v_ref, out_ref, buf_ref, tile_ref, sems, out_sems):
    size = k_ref.shape[0] // CHUNKS
    places = [pl.ds(t * size, size) for t in range(CHUNKS)]
    copies = []
    for t, rows in enumerate(places):
        for n, ref in enumerate((k_ref, v_ref)):
            copies.append(pltpu.make_async_copy(ref.at[rows], buf_ref.at[n, rows], sems.at[n, t]))
            copies[-1].start()
    sent = []
    for t, rows in enumerate(places):
        copies[2 * t].wait()
        copies[2 * t + 1].wait()
        fill_tiles(buf_ref.at[0, rows], buf_ref.at[1, rows], tile_ref, rows, repeat)
        sent.append(pltpu.make_async_copy(tile_ref.at[:, rows], out_ref.at[:, rows], out_sems.at[t]))
        sent[-1].start()
    for copy in sent:
        copy.wait()


def pack_queries_kernel(repeat, count, far, waits, q_ref, c_ref, *rest):
    rest = rest[waits:]
    out_refs, (buf_ref, tile_ref, sems, out_sems) = rest[:count], rest[count:]
    cols = sides((q_ref,), count)[far]
    copies = []
    for n, ref in enumerate((q_ref, c_ref)):
        copies.append(pltpu.make_async_copy(ref.at[:, cols], buf_ref.at[n], sems.at[n]))
        copies[-1].start()
    for copy in copies:
        copy.wait()
    fill_tiles(buf_ref.at[0], buf_ref.at[1], tile_ref, pl.ds(0, q_ref.shape[0]), repeat)
    for copy in send_far(tile_ref, out_refs, out_sems):
        copy.wait()


def unpack_kernel(repeat, in_ref, att_ref, dq_ref, dk_ref, dv_ref, buf_ref, sems):
    tokens, features = att_ref.shape
    size = tokens // CHUNKS
    copies = []
    for t in range(CHUNKS):
        rows = pl.ds(t * size, size)
        for half in range(2):
            place = pl.ds(half * tokens + t * size, size)
            for pair in range(features // PAIR):
                cols = pl.ds(pair * PAIR, PAIR)
                even = in_ref[2 * pair * repeat, place, :]
                odd = in_ref[(2 * pair + 1) * repeat, place, :]
                buf_ref[2 * half, rows, cols] = jnp.concatenate(
                    (even[:, :HEAD_DIM], odd[:, :HEAD_DIM]), axis=1
                )
                buf_ref[2 * half + 1, rows, cols] = jnp.concatenate(
                    (even[:, HEAD_DIM:], odd[:, HEAD_DIM:]), axis=1
                )
        for n, ref in enumerate((dq_ref, att_ref, dk_ref, dv_ref)):
            copies.append(pltpu.make_async_copy(buf_ref.at[n, rows], ref.at[rows], sems.at[n, t]))
            copies[-1].start()
    for copy in copies:
        copy.wait()


def attend(tables, kv_ref, acc_ref, blocks, group, items):
    glob_ref, owner_ref, local_ref = tables
    per_device = kv_ref.shape[0] // BLOCK // lax.axis_size("ctx")
    low = lax.broadcasted_iota(jnp.int32, (BLOCK, PAIR), 1) < HEAD_DIM
    place = lax.broadcasted_iota(jnp.int32, (1, SPAN), 1)

    def load(i, qc):
        ids = [jnp.maximum(i - 1, 0), i, jnp.minimum(i + 1, blocks - 1)]
        ids += [glob_ref[n] for n in range(GLOBALS)]
        for n in range(ROUNDS):
            entry = group * ROUNDS + n
            ids.append(owner_ref[entry, i] * per_device + local_ref[entry, i])
        rows = [pl.ds(pl.multiple_of(one * BLOCK, BLOCK), BLOCK) for one in ids]
        kv = jnp.concatenate([kv_ref[r, :] for r in rows], axis=0)
        zero = jnp.zeros_like(qc)
        return rows, kv, jnp.where(low, qc, zero), jnp.where(low, zero, qc)

    def products(kv, q_part, c_part):
        return lax.dot_general(
            jnp.concatenate((q_part, c_part), axis=0),
            kv,
            (((1,), (1,)), ((), ())),
            preferred_element_type=jnp.float32,
        )

    def softmax(i, both):
        absent = ((place < BLOCK) & (i == 0)) | (
            (place >= 2 * BLOCK) & (place < 3 * BLOCK) & (i == blocks - 1)
        )
        scores = jnp.where(absent, NEG_FILL, both[:BLOCK])
        dprob = both[BLOCK:]
        row_max = jnp.max(scores, axis=-1, keepdims=True)
        weights = jnp.exp2((scores - row_max) * EXP_SCALE)
        inverse = 1.0 / jnp.sum(weights, axis=-1, keepdims=True)
        row_dot = jnp.sum(weights * dprob, axis=-1, keepdims=True) * inverse
        probs = weights * inverse
        dscore = probs * (dprob - row_dot)
        return jnp.concatenate((probs.astype(jnp.bfloat16), dscore.astype(jnp.bfloat16)), axis=0)

    def query_side(kv, pd):
        res = jnp.dot(pd, kv, preferred_element_type=jnp.float32)
        return jnp.where(low, res[BLOCK:] * SCALE, res[:BLOCK]).astype(jnp.bfloat16)

    def key_side(q_part, c_part, pd):
        return lax.dot_general(
            pd,
            jnp.concatenate((c_part, q_part), axis=0),
            (((0,), (0,)), ((), ())),
            preferred_element_type=jnp.float32,
        )

    loaded = [load(i, qc) for i, qc, _ in items]
    both = [products(*one[1:]) for one in loaded]
    pds = [softmax(item[0], one) for item, one in zip(items, both)]
    terms = []
    for (_, kv, q_part, c_part), pd, item in zip(loaded, pds, items):
        item[2](query_side(kv, pd))
        terms.append(key_side(q_part, c_part, pd))
    for one, term in zip(loaded, terms):
        for n, r in enumerate(one[0]):
            acc_ref[r, :] += term[n * BLOCK : (n + 1) * BLOCK]


def my_group(repeat):
    return lax.axis_index("ctx") // (repeat * GROUP_HEADS)


def near_kernel(repeat, count, glob_ref, owner_ref, local_ref, kv_ref, *rest):
    qc_refs, (acc_ref, out_ref, near_ref) = rest[:count], rest[count:]
    tokens = qc_refs[0].shape[0]
    mine = lax.rem(lax.axis_index("ctx"), count)
    base = lax.axis_index("ctx") - mine
    blocks = kv_ref.shape[0] // BLOCK
    per_device = tokens // BLOCK
    acc_ref[...] = jnp.zeros_like(acc_ref)
    for m, ref in enumerate(qc_refs):
        near_ref[mine ^ m] = ref[...]

    def step(j):
        items = []
        for u in range(UNROLL):
            place = j * UNROLL + u
            device, local = lax.div(place, per_device), lax.rem(place, per_device)
            rows = pl.ds(pl.multiple_of(local * BLOCK, BLOCK), BLOCK)

            def put(value, device=device, rows=rows):
                out_ref[device, rows, :] = value

            items.append((base * per_device + place, near_ref[device, rows, :], put))
        attend((glob_ref, owner_ref, local_ref), kv_ref, acc_ref, blocks, my_group(repeat), items)

    pl.loop(0, count * per_device // UNROLL)(step)


def far_step(repeat, count, first, tables, kv_ref, qc_refs, acc_ref, out_refs):
    me = lax.axis_index("ctx")
    mine = lax.rem(me, count)
    base = me - mine
    items = []
    for m, (qc_ref, out_ref) in enumerate(zip(qc_refs, out_refs)):
        source = (count - base) + (mine ^ (first + m))
        per_device = qc_ref.shape[0] // BLOCK
        for local in range(per_device):
            rows = pl.ds(local * BLOCK, BLOCK)

            def put(value, out_ref=out_ref, rows=rows):
                out_ref[rows, :] = value

            items.append((source * per_device + local, qc_ref, rows, put))
    for start in range(0, len(items), UNROLL):
        now = [(i, ref[rows, :], put) for i, ref, rows, put in items[start : start + UNROLL]]
        attend(tables, kv_ref, acc_ref, kv_ref.shape[0] // BLOCK, my_group(repeat), now)


def far_kernel(repeat, count, first, size, glob_ref, owner_ref, local_ref, kv_ref, acc_in_ref, *rest):
    qc_refs, acc_ref, out_refs = rest[:size], rest[size], rest[size + 1 :]
    acc_ref[...] = acc_in_ref[...]
    far_step(repeat, count, first, (glob_ref, owner_ref, local_ref), kv_ref, qc_refs, acc_ref, out_refs)


def last_kernel(repeat, count, first, size, glob_ref, owner_ref, local_ref, kv_ref, acc_in_ref, *rest):
    qc_refs, near_ref, done_refs = rest[:size], rest[size], rest[size + 1 : -3]
    out_ref, acc_ref, late_ref = rest[-3:]
    tokens = qc_refs[0].shape[0]
    me = lax.axis_index("ctx")
    mine = lax.rem(me, count)
    base = me - mine
    acc_ref[...] = acc_in_ref[...]
    late = [late_ref.at[m] for m in range(size)]
    far_step(repeat, count, first, (glob_ref, owner_ref, local_ref), kv_ref, qc_refs, acc_ref, late)
    for j in range(count):
        out_ref[base + j, :tokens, :] = near_ref[j]
    for m, ref in enumerate(list(done_refs) + late):
        out_ref[(count - base) + (mine ^ m), :tokens, :] = ref[...]

    def finish(d):
        acc = acc_ref[pl.ds(pl.multiple_of(d * tokens, tokens), tokens), :]
        left = lax.broadcasted_iota(jnp.int32, acc.shape, 1) < HEAD_DIM
        out_ref[d, tokens:, :] = jnp.where(left, acc * SCALE, acc).astype(jnp.bfloat16)

    pl.loop(0, 2 * count)(finish)


def per_device(query, key, value, cotangent, global_ids, rand_owner, rand_local):
    tokens, features = query.shape
    heads = features // HEAD_DIM
    devices = lax.axis_size("ctx")
    repeat = max(1, devices // heads)
    count = devices // 2
    params = pltpu.CompilerParams(vmem_limit_bytes=24 << 20)
    roomy = pltpu.CompilerParams(vmem_limit_bytes=60 << 20)
    tile = jax.ShapeDtypeStruct((tokens, PAIR), jnp.bfloat16)

    packed = pl.pallas_call(
        functools.partial(pack_keys_kernel, repeat),
        out_shape=jax.ShapeDtypeStruct((devices, tokens, PAIR), jnp.bfloat16),
        in_specs=[HBM] * 2,
        out_specs=HBM,
        scratch_shapes=[
            pltpu.VMEM((2, tokens, features), jnp.bfloat16),
            pltpu.VMEM((devices, tokens, PAIR), jnp.bfloat16),
            pltpu.SemaphoreType.DMA((2, CHUNKS)),
            pltpu.SemaphoreType.DMA((CHUNKS,)),
        ],
        compiler_params=roomy,
    )(key, value)
    keys = lax.all_to_all(packed, "ctx", 0, 0, tiled=True).reshape(devices * tokens, PAIR)

    def swap(array, mask):
        return lax.ppermute(array, "ctx", [(i, i ^ mask) for i in range(devices)])

    def pack_queries(far, waits):
        return pl.pallas_call(
            functools.partial(pack_queries_kernel, repeat, count, far, len(waits)),
            out_shape=[tile] * count,
            in_specs=[HBM] * 2 + [pl.BlockSpec(memory_space=pl.ANY)] * len(waits),
            out_specs=[HBM] * count,
            scratch_shapes=[
                pltpu.VMEM((2, tokens, features // 2), jnp.bfloat16),
                pltpu.VMEM((count, tokens, PAIR), jnp.bfloat16),
                pltpu.SemaphoreType.DMA((2,)),
                pltpu.SemaphoreType.DMA((count,)),
            ],
            compiler_params=pltpu.CompilerParams(vmem_limit_bytes=16 << 20),
        )(query, cotangent, *waits)

    near_qc = pack_queries(0, [])
    near_qc = [one if m == 0 else swap(one, m) for m, one in enumerate(near_qc)]
    far_qc = pack_queries(1, [])
    far_qc = [swap(one, count + m) for m, one in enumerate(far_qc)]

    tables = (global_ids, rand_owner.T, rand_local.T)
    total = jax.ShapeDtypeStruct((devices * tokens, PAIR), jnp.float32)
    acc, near_out = pl.pallas_call(
        functools.partial(near_kernel, repeat, count),
        out_shape=[total, jax.ShapeDtypeStruct((count, tokens, PAIR), jnp.bfloat16)],
        in_specs=[SMEM] * 3 + [VMEM] * (1 + count),
        out_specs=[VMEM] * 2,
        scratch_shapes=[pltpu.VMEM((count, tokens, PAIR), jnp.bfloat16)],
        compiler_params=params,
        cost_estimate=pl.CostEstimate(flops=7 * 10**9, bytes_accessed=4 << 20, transcendentals=0),
    )(*tables, keys, *near_qc)
    done = []
    *sizes, size = [count * part // sum(PARTS) for part in PARTS]
    first = 0
    for some in sizes:
        acc, *outs = pl.pallas_call(
            functools.partial(far_kernel, repeat, count, first, some),
            out_shape=[total] + [tile] * some,
            in_specs=[SMEM] * 3 + [VMEM] * (2 + some),
            out_specs=[VMEM] * (1 + some),
            compiler_params=params,
            cost_estimate=pl.CostEstimate(flops=some * 10**9, bytes_accessed=4 << 20, transcendentals=0),
        )(*tables, keys, acc, *far_qc[first : first + some])
        done += outs
        first += some
    grads = pl.pallas_call(
        functools.partial(last_kernel, repeat, count, first, size),
        out_shape=jax.ShapeDtypeStruct((devices, 2 * tokens, PAIR), jnp.bfloat16),
        in_specs=[SMEM] * 3 + [VMEM] * (3 + count),
        out_specs=VMEM,
        scratch_shapes=[
            pltpu.VMEM((devices * tokens, PAIR), jnp.float32),
            pltpu.VMEM((size, tokens, PAIR), jnp.bfloat16),
        ],
        compiler_params=params,
    )(*tables, keys, acc, *far_qc[first:], near_out, *done)
    back = lax.all_to_all(grads, "ctx", 0, 0, tiled=True)
    return pl.pallas_call(
        functools.partial(unpack_kernel, repeat),
        out_shape=[jax.ShapeDtypeStruct((tokens, features), jnp.bfloat16)] * 4,
        in_specs=[VMEM],
        out_specs=[HBM] * 4,
        scratch_shapes=[
            pltpu.VMEM((4, tokens, features), jnp.bfloat16),
            pltpu.SemaphoreType.DMA((4, CHUNKS)),
        ],
        compiler_params=params,
    )(back)


def solution(mesh):
    split = P(("groups", "ctx"), None)
    return jax.shard_map(
        per_device,
        mesh=mesh,
        in_specs=(split, split, split, split, P("groups"), P("groups", None), P("groups", None)),
        out_specs=(split, split, split, split),
        check_vma=False,
    )
```

```python
import functools
import math

import jax
import jax.numpy as jnp
from jax import lax
from jax.experimental import pallas as pl
from jax.experimental.pallas import tpu as pltpu
from jax.sharding import PartitionSpec as P

HEAD_DIM = 64
GROUP_HEADS = 8
BLOCK = 64
GLOBALS = 2
ROUNDS = 3
KINDS = 3 + GLOBALS + ROUNDS
SPAN = KINDS * BLOCK
PAIR = 2 * HEAD_DIM
NEG_FILL = -1e30
UNROLL = 8
CHUNKS = 4
PARTS = (8, 4, 2, 2)
SCALE = HEAD_DIM ** -0.5
EXP_SCALE = SCALE * math.log2(math.e)
VMEM = pl.BlockSpec(memory_space=pltpu.VMEM)
SMEM = pl.BlockSpec(memory_space=pltpu.SMEM)
HBM = pl.BlockSpec(memory_space=pltpu.HBM)


def halves(first, second):
    even = jnp.concatenate((first[:, :HEAD_DIM], second[:, :HEAD_DIM]), axis=1)
    odd = jnp.concatenate((first[:, HEAD_DIM:], second[:, HEAD_DIM:]), axis=1)
    return even, odd


def fill_tiles(first_ref, second_ref, tile_ref, place, repeat):
    for pair in range(first_ref.shape[-1] // PAIR):
        cols = pl.ds(pair * PAIR, PAIR)
        even, odd = halves(first_ref[:, cols], second_ref[:, cols])
        for n in range(repeat):
            tile_ref[2 * pair * repeat + n, place, :] = even
            tile_ref[(2 * pair + 1) * repeat + n, place, :] = odd


def send_far(tile_ref, far_refs, sems):
    count = len(far_refs)
    mine = lax.rem(lax.axis_index("ctx"), count)
    copies = []
    for m, ref in enumerate(far_refs):
        copies.append(pltpu.make_async_copy(tile_ref.at[mine ^ m], ref, sems.at[m]))
        copies[-1].start()
    return copies


def sides(refs, count):
    width = refs[0].shape[1] // 2
    upper = lax.div(lax.axis_index("ctx"), count)
    near = pl.ds(pl.multiple_of(upper * width, PAIR), width)
    far = pl.ds(pl.multiple_of((1 - upper) * width, PAIR), width)
    return near, far


def pack_keys_kernel(repeat, k_ref, v_ref, out_ref, buf_ref, tile_ref, sems, out_sems):
    size = k_ref.shape[0] // CHUNKS
    places = [pl.ds(t * size, size) for t in range(CHUNKS)]
    copies = []
    for t, rows in enumerate(places):
        for n, ref in enumerate((k_ref, v_ref)):
            copies.append(pltpu.make_async_copy(ref.at[rows], buf_ref.at[n, rows], sems.at[n, t]))
            copies[-1].start()
    sent = []
    for t, rows in enumerate(places):
        copies[2 * t].wait()
        copies[2 * t + 1].wait()
        fill_tiles(buf_ref.at[0, rows], buf_ref.at[1, rows], tile_ref, rows, repeat)
        sent.append(pltpu.make_async_copy(tile_ref.at[:, rows], out_ref.at[:, rows], out_sems.at[t]))
        sent[-1].start()
    for copy in sent:
        copy.wait()


def pack_queries_kernel(repeat, count, far, waits, q_ref, c_ref, *rest):
    rest = rest[waits:]
    out_refs, (buf_ref, tile_ref, sems, out_sems) = rest[:count], rest[count:]
    cols = sides((q_ref,), count)[far]
    copies = []
    for n, ref in enumerate((q_ref, c_ref)):
        copies.append(pltpu.make_async_copy(ref.at[:, cols], buf_ref.at[n], sems.at[n]))
        copies[-1].start()
    for copy in copies:
        copy.wait()
    fill_tiles(buf_ref.at[0], buf_ref.at[1], tile_ref, pl.ds(0, q_ref.shape[0]), repeat)
    for copy in send_far(tile_ref, out_refs, out_sems):
        copy.wait()


def unpack_kernel(repeat, in_ref, att_ref, dq_ref, dk_ref, dv_ref, buf_ref, sems):
    tokens, features = att_ref.shape
    size = tokens // CHUNKS
    copies = []
    for t in range(CHUNKS):
        rows = pl.ds(t * size, size)
        for half in range(2):
            place = pl.ds(half * tokens + t * size, size)
            for pair in range(features // PAIR):
                cols = pl.ds(pair * PAIR, PAIR)
                even = in_ref[2 * pair * repeat, place, :]
                odd = in_ref[(2 * pair + 1) * repeat, place, :]
                buf_ref[2 * half, rows, cols] = jnp.concatenate(
                    (even[:, :HEAD_DIM], odd[:, :HEAD_DIM]), axis=1
                )
                buf_ref[2 * half + 1, rows, cols] = jnp.concatenate(
                    (even[:, HEAD_DIM:], odd[:, HEAD_DIM:]), axis=1
                )
        for n, ref in enumerate((dq_ref, att_ref, dk_ref, dv_ref)):
            copies.append(pltpu.make_async_copy(buf_ref.at[n, rows], ref.at[rows], sems.at[n, t]))
            copies[-1].start()
    for copy in copies:
        copy.wait()


def attend(table_ref, kv_ref, acc_ref, repeat, items):
    blocks = kv_ref.shape[0] // BLOCK
    group = lax.axis_index("ctx") // (repeat * GROUP_HEADS)
    globals_at = table_ref.shape[0] - GLOBALS
    low = lax.broadcasted_iota(jnp.int32, (BLOCK, PAIR), 1) < HEAD_DIM
    place = lax.broadcasted_iota(jnp.int32, (1, SPAN), 1)

    def load(i, qc):
        ids = [jnp.maximum(i - 1, 0), i, jnp.minimum(i + 1, blocks - 1)]
        ids += [table_ref[globals_at + n] for n in range(GLOBALS)]
        ids += [table_ref[(group * ROUNDS + n) * blocks + i] for n in range(ROUNDS)]
        rows = [pl.ds(pl.multiple_of(one * BLOCK, BLOCK), BLOCK) for one in ids]
        kv = jnp.concatenate([kv_ref[r, :] for r in rows], axis=0)
        zero = jnp.zeros_like(qc)
        return rows, kv, jnp.where(low, qc, zero), jnp.where(low, zero, qc)

    def products(kv, q_part, c_part):
        return lax.dot_general(
            jnp.concatenate((q_part, c_part), axis=0),
            kv,
            (((1,), (1,)), ((), ())),
            preferred_element_type=jnp.float32,
        )

    def softmax(i, both):
        absent = ((place < BLOCK) & (i == 0)) | (
            (place >= 2 * BLOCK) & (place < 3 * BLOCK) & (i == blocks - 1)
        )
        scores = jnp.where(absent, NEG_FILL, both[:BLOCK])
        dprob = both[BLOCK:]
        row_max = jnp.max(scores, axis=-1, keepdims=True)
        weights = jnp.exp2((scores - row_max) * EXP_SCALE)
        inverse = 1.0 / jnp.sum(weights, axis=-1, keepdims=True)
        row_dot = jnp.sum(weights * dprob, axis=-1, keepdims=True) * inverse
        probs = weights * inverse
        dscore = probs * (dprob - row_dot)
        return jnp.concatenate((probs.astype(jnp.bfloat16), dscore.astype(jnp.bfloat16)), axis=0)

    def query_side(kv, pd):
        res = jnp.dot(pd, kv, preferred_element_type=jnp.float32)
        return jnp.where(low, res[BLOCK:] * SCALE, res[:BLOCK]).astype(jnp.bfloat16)

    def key_side(q_part, c_part, pd):
        return lax.dot_general(
            pd,
            jnp.concatenate((c_part, q_part), axis=0),
            (((0,), (0,)), ((), ())),
            preferred_element_type=jnp.float32,
        )

    loaded = [load(i, qc) for i, qc, _ in items]
    both = [products(*one[1:]) for one in loaded]
    pds = [softmax(item[0], one) for item, one in zip(items, both)]
    terms = []
    for (_, kv, q_part, c_part), pd, item in zip(loaded, pds, items):
        item[2](query_side(kv, pd))
        terms.append(key_side(q_part, c_part, pd))
    for one, term in zip(loaded, terms):
        for n, r in enumerate(one[0]):
            acc_ref[r, :] += term[n * BLOCK : (n + 1) * BLOCK]


def attend_tiles(repeat, first, table_ref, kv_ref, acc_ref, qc_refs, out_refs):
    per_device = qc_refs[0].shape[0] // BLOCK
    items = []
    for m, (qc_ref, out_ref) in enumerate(zip(qc_refs, out_refs)):
        source = lax.axis_index("ctx") ^ (first + m)
        for local in range(per_device):
            rows = pl.ds(local * BLOCK, BLOCK)

            def put(value, out_ref=out_ref, rows=rows):
                out_ref[rows, :] = value

            items.append((source * per_device + local, qc_ref, rows, put))
    for start in range(0, len(items), UNROLL):
        now = [(i, ref[rows, :], put) for i, ref, rows, put in items[start : start + UNROLL]]
        attend(table_ref, kv_ref, acc_ref, repeat, now)


def part_kernel(repeat, first, size, table_ref, kv_ref, *rest):
    acc_in_refs, rest = rest[: first > 0], rest[first > 0 :]
    qc_refs, acc_ref, out_refs = rest[:size], rest[size], rest[size + 1 :]
    acc_ref[...] = acc_in_refs[0][...] if first else jnp.zeros_like(acc_ref)
    attend_tiles(repeat, first, table_ref, kv_ref, acc_ref, qc_refs, out_refs)


def last_kernel(repeat, first, size, table_ref, kv_ref, acc_in_ref, *rest):
    qc_refs, done_refs, (out_ref, acc_ref, late_ref) = rest[:size], rest[size:-3], rest[-3:]
    tokens = qc_refs[0].shape[0]
    acc_ref[...] = acc_in_ref[...]
    late = [late_ref.at[m] for m in range(size)]
    attend_tiles(repeat, first, table_ref, kv_ref, acc_ref, qc_refs, late)
    for m, ref in enumerate(list(done_refs) + late):
        out_ref[lax.axis_index("ctx") ^ m, :tokens, :] = ref[...]

    def finish(d):
        acc = acc_ref[pl.ds(pl.multiple_of(d * tokens, tokens), tokens), :]
        left = lax.broadcasted_iota(jnp.int32, acc.shape, 1) < HEAD_DIM
        out_ref[d, tokens:, :] = jnp.where(left, acc * SCALE, acc).astype(jnp.bfloat16)

    pl.loop(0, out_ref.shape[0])(finish)


def per_device(query, key, value, cotangent, global_ids, rand_owner, rand_local):
    tokens, features = query.shape
    heads = features // HEAD_DIM
    devices = lax.axis_size("ctx")
    repeat = max(1, devices // heads)
    count = devices // 2
    params = pltpu.CompilerParams(vmem_limit_bytes=24 << 20)
    roomy = pltpu.CompilerParams(vmem_limit_bytes=60 << 20)
    tile = jax.ShapeDtypeStruct((tokens, PAIR), jnp.bfloat16)

    packed = pl.pallas_call(
        functools.partial(pack_keys_kernel, repeat),
        out_shape=jax.ShapeDtypeStruct((devices, tokens, PAIR), jnp.bfloat16),
        in_specs=[HBM] * 2,
        out_specs=HBM,
        scratch_shapes=[
            pltpu.VMEM((2, tokens, features), jnp.bfloat16),
            pltpu.VMEM((devices, tokens, PAIR), jnp.bfloat16),
            pltpu.SemaphoreType.DMA((2, CHUNKS)),
            pltpu.SemaphoreType.DMA((CHUNKS,)),
        ],
        compiler_params=roomy,
    )(key, value)
    keys = lax.all_to_all(packed, "ctx", 0, 0, tiled=True).reshape(devices * tokens, PAIR)

    def swap(array, mask):
        return lax.ppermute(array, "ctx", [(i, i ^ mask) for i in range(devices)])

    def pack_queries(far, waits):
        return pl.pallas_call(
            functools.partial(pack_queries_kernel, repeat, count, far, len(waits)),
            out_shape=[tile] * count,
            in_specs=[HBM] * 2 + [pl.BlockSpec(memory_space=pl.ANY)] * len(waits),
            out_specs=[HBM] * count,
            scratch_shapes=[
                pltpu.VMEM((2, tokens, features // 2), jnp.bfloat16),
                pltpu.VMEM((count, tokens, PAIR), jnp.bfloat16),
                pltpu.SemaphoreType.DMA((2,)),
                pltpu.SemaphoreType.DMA((count,)),
            ],
            compiler_params=pltpu.CompilerParams(vmem_limit_bytes=16 << 20),
        )(query, cotangent, *waits)

    near_qc = pack_queries(0, [])
    near_qc = [one if m == 0 else swap(one, m) for m, one in enumerate(near_qc)]
    far_qc = pack_queries(1, [])
    far_qc = [swap(one, count + m) for m, one in enumerate(far_qc)]

    picked = (rand_owner * (tokens // BLOCK) + rand_local).T.reshape(-1)
    table = jnp.concatenate((picked, global_ids))
    total = jax.ShapeDtypeStruct((devices * tokens, PAIR), jnp.float32)
    *sizes, last = [devices * part // sum(PARTS) for part in PARTS]
    qc = near_qc + far_qc
    acc, done = [], []
    for size in sizes:
        first = len(done)
        outs = pl.pallas_call(
            functools.partial(part_kernel, repeat, first, size),
            out_shape=[total] + [tile] * size,
            in_specs=[SMEM] + [VMEM] * (1 + len(acc) + size),
            out_specs=[VMEM] * (1 + size),
            compiler_params=params,
            cost_estimate=pl.CostEstimate(flops=size * 10**9, bytes_accessed=4 << 20, transcendentals=0),
        )(table, keys, *acc, *qc[first : first + size])
        acc = [outs[0]]
        done += outs[1:]
    first = len(done)
    grads = pl.pallas_call(
        functools.partial(last_kernel, repeat, first, last),
        out_shape=jax.ShapeDtypeStruct((devices, 2 * tokens, PAIR), jnp.bfloat16),
        in_specs=[SMEM] + [VMEM] * (2 + devices),
        out_specs=VMEM,
        scratch_shapes=[
            pltpu.VMEM((devices * tokens, PAIR), jnp.float32),
            pltpu.VMEM((last, tokens, PAIR), jnp.bfloat16),
        ],
        compiler_params=params,
    )(table, keys, *acc, *qc[first:], *done)
    back = lax.all_to_all(grads, "ctx", 0, 0, tiled=True)
    return pl.pallas_call(
        functools.partial(unpack_kernel, repeat),
        out_shape=[jax.ShapeDtypeStruct((tokens, features), jnp.bfloat16)] * 4,
        in_specs=[VMEM],
        out_specs=[HBM] * 4,
        scratch_shapes=[
            pltpu.VMEM((4, tokens, features), jnp.bfloat16),
            pltpu.SemaphoreType.DMA((4, CHUNKS)),
        ],
        compiler_params=params,
    )(back)


def solution(mesh):
    split = P(("groups", "ctx"), None)
    return jax.shard_map(
        per_device,
        mesh=mesh,
        in_specs=(split, split, split, split, P("groups"), P("groups", None), P("groups", None)),
        out_specs=(split, split, split, split),
        check_vma=False,
    )
```

```python
import functools
import math

import jax
import jax.numpy as jnp
from jax import lax
from jax.experimental import pallas as pl
from jax.experimental.pallas import tpu as pltpu
from jax.sharding import PartitionSpec as P

HEAD_DIM = 64
GROUP_HEADS = 8
BLOCK = 64
GLOBALS = 2
ROUNDS = 3
KINDS = 3 + GLOBALS + ROUNDS
SPAN = KINDS * BLOCK
PAIR = 2 * HEAD_DIM
NEG_FILL = -1e30
UNROLL = 8
CHUNKS = 4
EARLY = 4
PARTS = (8, 4, 2, 2)
SCALE = HEAD_DIM ** -0.5
EXP_SCALE = SCALE * math.log2(math.e)
VMEM = pl.BlockSpec(memory_space=pltpu.VMEM)
SMEM = pl.BlockSpec(memory_space=pltpu.SMEM)
HBM = pl.BlockSpec(memory_space=pltpu.HBM)


def halves(first, second):
    even = jnp.concatenate((first[:, :HEAD_DIM], second[:, :HEAD_DIM]), axis=1)
    odd = jnp.concatenate((first[:, HEAD_DIM:], second[:, HEAD_DIM:]), axis=1)
    return even, odd


def fill_tiles(first_ref, second_ref, tile_ref, place, repeat):
    for pair in range(first_ref.shape[-1] // PAIR):
        cols = pl.ds(pair * PAIR, PAIR)
        even, odd = halves(first_ref[:, cols], second_ref[:, cols])
        for n in range(repeat):
            tile_ref[2 * pair * repeat + n, place, :] = even
            tile_ref[(2 * pair + 1) * repeat + n, place, :] = odd


def send_far(tile_ref, far_refs, sems):
    count = len(far_refs)
    mine = lax.rem(lax.axis_index("ctx"), count)
    copies = []
    for m, ref in enumerate(far_refs):
        copies.append(pltpu.make_async_copy(tile_ref.at[mine ^ m], ref, sems.at[m]))
        copies[-1].start()
    return copies


def sides(refs, count):
    width = refs[0].shape[1] // 2
    upper = lax.div(lax.axis_index("ctx"), count)
    near = pl.ds(pl.multiple_of(upper * width, PAIR), width)
    far = pl.ds(pl.multiple_of((1 - upper) * width, PAIR), width)
    return near, far


def pack_keys_kernel(repeat, k_ref, v_ref, out_ref, buf_ref, tile_ref, sems, out_sems):
    size = k_ref.shape[0] // CHUNKS
    places = [pl.ds(t * size, size) for t in range(CHUNKS)]
    copies = []
    for t, rows in enumerate(places):
        for n, ref in enumerate((k_ref, v_ref)):
            copies.append(pltpu.make_async_copy(ref.at[rows], buf_ref.at[n, rows], sems.at[n, t]))
            copies[-1].start()
    sent = []
    for t, rows in enumerate(places):
        copies[2 * t].wait()
        copies[2 * t + 1].wait()
        fill_tiles(buf_ref.at[0, rows], buf_ref.at[1, rows], tile_ref, rows, repeat)
        sent.append(pltpu.make_async_copy(tile_ref.at[:, rows], out_ref.at[:, rows], out_sems.at[t]))
        sent[-1].start()
    for copy in sent:
        copy.wait()


def pack_queries_kernel(repeat, count, far, waits, q_ref, c_ref, *rest):
    rest = rest[waits:]
    out_refs, (buf_ref, tile_ref, sems, out_sems) = rest[:count], rest[count:]
    cols = sides((q_ref,), count)[far]
    copies = []
    for n, ref in enumerate((q_ref, c_ref)):
        copies.append(pltpu.make_async_copy(ref.at[:, cols], buf_ref.at[n], sems.at[n]))
        copies[-1].start()
    for copy in copies:
        copy.wait()
    fill_tiles(buf_ref.at[0], buf_ref.at[1], tile_ref, pl.ds(0, q_ref.shape[0]), repeat)
    for copy in send_far(tile_ref, out_refs, out_sems):
        copy.wait()


def hold_kernel(count, *refs):
    for source, ref in zip(refs[:count], refs[-count:]):
        ref[...] = source[...]


def unpack_kernel(repeat, keys_ref, *rest):
    tile_refs, rest = rest[:-7], rest[-7:]
    (att_ref, dq_ref, dk_ref, dv_ref), (tiles_ref, buf_ref, sems) = rest[:4], rest[4:]
    tokens, features = att_ref.shape
    size = tokens // CHUNKS
    me = lax.axis_index("ctx")
    copies = []

    def write(in_ref, first, refs):
        for t in range(CHUNKS):
            rows = pl.ds(t * size, size)
            for pair in range(features // PAIR):
                cols = pl.ds(pair * PAIR, PAIR)
                low, high = halves(in_ref[2 * pair * repeat, rows, :], in_ref[(2 * pair + 1) * repeat, rows, :])
                buf_ref[first, rows, cols] = low
                buf_ref[first + 1, rows, cols] = high
            for n, ref in enumerate(refs):
                copies.append(
                    pltpu.make_async_copy(buf_ref.at[first + n, rows], ref.at[rows], sems.at[first + n, t])
                )
                copies[-1].start()

    write(keys_ref, 0, (dk_ref, dv_ref))
    for m, ref in enumerate(tile_refs):
        tiles_ref[me ^ m] = ref[...]
    write(tiles_ref, 2, (dq_ref, att_ref))
    for copy in copies:
        copy.wait()


def attend(table_ref, kv_ref, acc_ref, repeat, items):
    blocks = kv_ref.shape[0] // BLOCK
    group = lax.axis_index("ctx") // (repeat * GROUP_HEADS)
    globals_at = table_ref.shape[0] - GLOBALS
    low = lax.broadcasted_iota(jnp.int32, (BLOCK, PAIR), 1) < HEAD_DIM
    place = lax.broadcasted_iota(jnp.int32, (1, SPAN), 1)

    def load(i, qc):
        ids = [jnp.maximum(i - 1, 0), i, jnp.minimum(i + 1, blocks - 1)]
        ids += [table_ref[globals_at + n] for n in range(GLOBALS)]
        ids += [table_ref[(group * ROUNDS + n) * blocks + i] for n in range(ROUNDS)]
        rows = [pl.ds(pl.multiple_of(one * BLOCK, BLOCK), BLOCK) for one in ids]
        kv = jnp.concatenate([kv_ref[r, :] for r in rows], axis=0)
        zero = jnp.zeros_like(qc)
        return rows, kv, jnp.where(low, qc, zero), jnp.where(low, zero, qc)

    def products(kv, q_part, c_part):
        return lax.dot_general(
            jnp.concatenate((q_part, c_part), axis=0),
            kv,
            (((1,), (1,)), ((), ())),
            preferred_element_type=jnp.float32,
        )

    def softmax(i, both):
        absent = ((place < BLOCK) & (i == 0)) | (
            (place >= 2 * BLOCK) & (place < 3 * BLOCK) & (i == blocks - 1)
        )
        scores = jnp.where(absent, NEG_FILL, both[:BLOCK])
        dprob = both[BLOCK:]
        row_max = jnp.max(scores, axis=-1, keepdims=True)
        weights = jnp.exp2((scores - row_max) * EXP_SCALE)
        inverse = 1.0 / jnp.sum(weights, axis=-1, keepdims=True)
        row_dot = jnp.sum(weights * dprob, axis=-1, keepdims=True) * inverse
        probs = weights * inverse
        dscore = probs * (dprob - row_dot)
        return jnp.concatenate((probs.astype(jnp.bfloat16), dscore.astype(jnp.bfloat16)), axis=0)

    def query_side(kv, pd):
        res = jnp.dot(pd, kv, preferred_element_type=jnp.float32)
        return jnp.where(low, res[BLOCK:] * SCALE, res[:BLOCK]).astype(jnp.bfloat16)

    def key_side(q_part, c_part, pd):
        return lax.dot_general(
            pd,
            jnp.concatenate((c_part, q_part), axis=0),
            (((0,), (0,)), ((), ())),
            preferred_element_type=jnp.float32,
        )

    loaded = [load(i, qc) for i, qc, _ in items]
    both = [products(*one[1:]) for one in loaded]
    pds = [softmax(item[0], one) for item, one in zip(items, both)]
    terms = []
    for (_, kv, q_part, c_part), pd, item in zip(loaded, pds, items):
        item[2](query_side(kv, pd))
        terms.append(key_side(q_part, c_part, pd))
    for one, term in zip(loaded, terms):
        for n, r in enumerate(one[0]):
            acc_ref[r, :] += term[n * BLOCK : (n + 1) * BLOCK]


def attend_tiles(repeat, first, table_ref, kv_ref, acc_ref, qc_refs, out_refs):
    per_device = qc_refs[0].shape[0] // BLOCK
    items = []
    for m, (qc_ref, out_ref) in enumerate(zip(qc_refs, out_refs)):
        source = lax.axis_index("ctx") ^ (first + m)
        for local in range(per_device):
            rows = pl.ds(local * BLOCK, BLOCK)

            def put(value, out_ref=out_ref, rows=rows):
                out_ref[rows, :] = value

            items.append((source * per_device + local, qc_ref, rows, put))
    for start in range(0, len(items), UNROLL):
        now = [(i, ref[rows, :], put) for i, ref, rows, put in items[start : start + UNROLL]]
        attend(table_ref, kv_ref, acc_ref, repeat, now)


def part_kernel(repeat, first, size, table_ref, kv_ref, *rest):
    acc_in_refs, rest = rest[: first > 0], rest[first > 0 :]
    qc_refs, acc_ref, out_refs = rest[:size], rest[size], rest[size + 1 :]
    acc_ref[...] = acc_in_refs[0][...] if first else jnp.zeros_like(acc_ref)
    attend_tiles(repeat, first, table_ref, kv_ref, acc_ref, qc_refs, out_refs)


def last_kernel(repeat, first, size, table_ref, kv_ref, acc_in_ref, *rest):
    qc_refs, keys_ref, out_refs, acc_ref = rest[:size], rest[size], rest[size + 1 : -1], rest[-1]
    tokens = qc_refs[0].shape[0]
    acc_ref[...] = acc_in_ref[...]
    attend_tiles(repeat, first, table_ref, kv_ref, acc_ref, qc_refs, out_refs)

    def finish(d):
        acc = acc_ref[pl.ds(pl.multiple_of(d * tokens, tokens), tokens), :]
        left = lax.broadcasted_iota(jnp.int32, acc.shape, 1) < HEAD_DIM
        keys_ref[d] = jnp.where(left, acc * SCALE, acc).astype(jnp.bfloat16)

    pl.loop(0, keys_ref.shape[0])(finish)


def per_device(query, key, value, cotangent, global_ids, rand_owner, rand_local):
    tokens, features = query.shape
    heads = features // HEAD_DIM
    devices = lax.axis_size("ctx")
    repeat = max(1, devices // heads)
    count = devices // 2
    params = pltpu.CompilerParams(vmem_limit_bytes=24 << 20)
    roomy = pltpu.CompilerParams(vmem_limit_bytes=60 << 20)
    tile = jax.ShapeDtypeStruct((tokens, PAIR), jnp.bfloat16)

    packed = pl.pallas_call(
        functools.partial(pack_keys_kernel, repeat),
        out_shape=jax.ShapeDtypeStruct((devices, tokens, PAIR), jnp.bfloat16),
        in_specs=[HBM] * 2,
        out_specs=HBM,
        scratch_shapes=[
            pltpu.VMEM((2, tokens, features), jnp.bfloat16),
            pltpu.VMEM((devices, tokens, PAIR), jnp.bfloat16),
            pltpu.SemaphoreType.DMA((2, CHUNKS)),
            pltpu.SemaphoreType.DMA((CHUNKS,)),
        ],
        compiler_params=roomy,
    )(key, value)
    keys = lax.all_to_all(packed, "ctx", 0, 0, tiled=True).reshape(devices * tokens, PAIR)

    def swap(array, mask):
        return lax.ppermute(array, "ctx", [(i, i ^ mask) for i in range(devices)])

    def pack_queries(far, waits):
        return pl.pallas_call(
            functools.partial(pack_queries_kernel, repeat, count, far, len(waits)),
            out_shape=[tile] * count,
            in_specs=[HBM] * 2 + [pl.BlockSpec(memory_space=pl.ANY)] * len(waits),
            out_specs=[HBM] * count,
            scratch_shapes=[
                pltpu.VMEM((2, tokens, features // 2), jnp.bfloat16),
                pltpu.VMEM((count, tokens, PAIR), jnp.bfloat16),
                pltpu.SemaphoreType.DMA((2,)),
                pltpu.SemaphoreType.DMA((count,)),
            ],
            compiler_params=pltpu.CompilerParams(vmem_limit_bytes=16 << 20),
        )(query, cotangent, *waits)

    near_qc = pack_queries(0, [])
    near_qc = [one if m == 0 else swap(one, m) for m, one in enumerate(near_qc)]
    far_qc = pack_queries(1, [])
    far_qc = [swap(one, count + m) for m, one in enumerate(far_qc)]

    picked = (rand_owner * (tokens // BLOCK) + rand_local).T.reshape(-1)
    table = jnp.concatenate((picked, global_ids))
    total = jax.ShapeDtypeStruct((devices * tokens, PAIR), jnp.float32)
    *sizes, last = [devices * part // sum(PARTS) for part in PARTS]
    qc = near_qc + far_qc
    acc, done = [], []
    for size in sizes:
        first = len(done)
        outs = pl.pallas_call(
            functools.partial(part_kernel, repeat, first, size),
            out_shape=[total] + [tile] * size,
            in_specs=[SMEM] + [VMEM] * (1 + len(acc) + size),
            out_specs=[VMEM] * (1 + size),
            compiler_params=params,
            cost_estimate=pl.CostEstimate(flops=size * 10**9, bytes_accessed=4 << 20, transcendentals=0),
        )(table, keys, *acc, *qc[first : first + size])
        acc = [outs[0]]
        done += outs[1:]
    first = len(done)
    keys_out, *outs = pl.pallas_call(
        functools.partial(last_kernel, repeat, first, last),
        out_shape=[jax.ShapeDtypeStruct((devices, tokens, PAIR), jnp.bfloat16)] + [tile] * last,
        in_specs=[SMEM] + [VMEM] * (2 + last),
        out_specs=[VMEM] * (1 + last),
        scratch_shapes=[pltpu.VMEM((devices * tokens, PAIR), jnp.float32)],
        compiler_params=params,
    )(table, keys, *acc, *qc[first:])
    back = lax.all_to_all(keys_out, "ctx", 0, 0, tiled=True)
    split = count + EARLY * devices // sum(PARTS)
    early = [swap(one, count + m) for m, one in enumerate(done[count:split])]
    held = done[1:count] + done[split:] + outs
    held = pl.pallas_call(
        functools.partial(hold_kernel, len(held)),
        out_shape=[tile] * len(held),
        in_specs=[VMEM] * len(held) + [pl.BlockSpec(memory_space=pl.ANY)] * len(early),
        out_specs=[VMEM] * len(held),
        compiler_params=params,
        cost_estimate=pl.CostEstimate(flops=10**11, bytes_accessed=1 << 20, transcendentals=0),
    )(*held, *early)
    masks = list(range(1, count)) + list(range(split, devices))
    held = [swap(one, mask) for one, mask in zip(held, masks)]
    tiles = done[:1] + held[: count - 1] + early + held[count - 1 :]
    return pl.pallas_call(
        functools.partial(unpack_kernel, repeat),
        out_shape=[jax.ShapeDtypeStruct((tokens, features), jnp.bfloat16)] * 4,
        in_specs=[VMEM] * (1 + devices),
        out_specs=[HBM] * 4,
        scratch_shapes=[
            pltpu.VMEM((devices, tokens, PAIR), jnp.bfloat16),
            pltpu.VMEM((4, tokens, features), jnp.bfloat16),
            pltpu.SemaphoreType.DMA((4, CHUNKS)),
        ],
        compiler_params=params,
    )(back, *tiles)


def solution(mesh):
    split = P(("groups", "ctx"), None)
    return jax.shard_map(
        per_device,
        mesh=mesh,
        in_specs=(split, split, split, split, P("groups"), P("groups", None), P("groups", None)),
        out_specs=(split, split, split, split),
        check_vma=False,
    )
```

```python
import functools
import math

import jax
import jax.numpy as jnp
from jax import lax
from jax.experimental import pallas as pl
from jax.experimental.pallas import tpu as pltpu
from jax.sharding import PartitionSpec as P

HEAD_DIM = 64
GROUP_HEADS = 8
BLOCK = 64
GLOBALS = 2
ROUNDS = 3
KINDS = 3 + GLOBALS + ROUNDS
SPAN = KINDS * BLOCK
PAIR = 2 * HEAD_DIM
NEG_FILL = -1e30
UNROLL = 8
CHUNKS = 4
EARLY = 5
PARTS = (8, 5, 3)
SCALE = HEAD_DIM ** -0.5
EXP_SCALE = SCALE * math.log2(math.e)
VMEM = pl.BlockSpec(memory_space=pltpu.VMEM)
SMEM = pl.BlockSpec(memory_space=pltpu.SMEM)
HBM = pl.BlockSpec(memory_space=pltpu.HBM)


def halves(first, second):
    even = jnp.concatenate((first[:, :HEAD_DIM], second[:, :HEAD_DIM]), axis=1)
    odd = jnp.concatenate((first[:, HEAD_DIM:], second[:, HEAD_DIM:]), axis=1)
    return even, odd


def fill_tiles(first_ref, second_ref, tile_ref, place, repeat):
    for pair in range(first_ref.shape[-1] // PAIR):
        cols = pl.ds(pair * PAIR, PAIR)
        even, odd = halves(first_ref[:, cols], second_ref[:, cols])
        for n in range(repeat):
            tile_ref[2 * pair * repeat + n, place, :] = even
            tile_ref[(2 * pair + 1) * repeat + n, place, :] = odd


def send_far(tile_ref, far_refs, sems):
    count = len(far_refs)
    mine = lax.rem(lax.axis_index("ctx"), count)
    copies = []
    for m, ref in enumerate(far_refs):
        copies.append(pltpu.make_async_copy(tile_ref.at[mine ^ m], ref, sems.at[m]))
        copies[-1].start()
    return copies


def sides(refs, count):
    width = refs[0].shape[1] // 2
    upper = lax.div(lax.axis_index("ctx"), count)
    near = pl.ds(pl.multiple_of(upper * width, PAIR), width)
    far = pl.ds(pl.multiple_of((1 - upper) * width, PAIR), width)
    return near, far


def pack_keys_kernel(repeat, k_ref, v_ref, out_ref, buf_ref, tile_ref, sems, out_sems):
    size = k_ref.shape[0] // CHUNKS
    places = [pl.ds(t * size, size) for t in range(CHUNKS)]
    copies = []
    for t, rows in enumerate(places):
        for n, ref in enumerate((k_ref, v_ref)):
            copies.append(pltpu.make_async_copy(ref.at[rows], buf_ref.at[n, rows], sems.at[n, t]))
            copies[-1].start()
    sent = []
    for t, rows in enumerate(places):
        copies[2 * t].wait()
        copies[2 * t + 1].wait()
        fill_tiles(buf_ref.at[0, rows], buf_ref.at[1, rows], tile_ref, rows, repeat)
        sent.append(pltpu.make_async_copy(tile_ref.at[:, rows], out_ref.at[:, rows], out_sems.at[t]))
        sent[-1].start()
    for copy in sent:
        copy.wait()


def pack_queries_kernel(repeat, count, far, waits, q_ref, c_ref, *rest):
    rest = rest[waits:]
    out_refs, (buf_ref, tile_ref, sems, out_sems) = rest[:count], rest[count:]
    cols = sides((q_ref,), count)[far]
    copies = []
    for n, ref in enumerate((q_ref, c_ref)):
        copies.append(pltpu.make_async_copy(ref.at[:, cols], buf_ref.at[n], sems.at[n]))
        copies[-1].start()
    for copy in copies:
        copy.wait()
    fill_tiles(buf_ref.at[0], buf_ref.at[1], tile_ref, pl.ds(0, q_ref.shape[0]), repeat)
    for copy in send_far(tile_ref, out_refs, out_sems):
        copy.wait()


def hold_kernel(count, *refs):
    for source, ref in zip(refs[:count], refs[-count:]):
        ref[...] = source[...]


def unpack_kernel(repeat, keys_ref, *rest):
    tile_refs, rest = rest[:-7], rest[-7:]
    (att_ref, dq_ref, dk_ref, dv_ref), (tiles_ref, buf_ref, sems) = rest[:4], rest[4:]
    tokens, features = att_ref.shape
    size = tokens // CHUNKS
    me = lax.axis_index("ctx")
    copies = []

    def write(in_ref, first, refs):
        for t in range(CHUNKS):
            rows = pl.ds(t * size, size)
            for pair in range(features // PAIR):
                cols = pl.ds(pair * PAIR, PAIR)
                low, high = halves(in_ref[2 * pair * repeat, rows, :], in_ref[(2 * pair + 1) * repeat, rows, :])
                buf_ref[first, rows, cols] = low
                buf_ref[first + 1, rows, cols] = high
            for n, ref in enumerate(refs):
                copies.append(
                    pltpu.make_async_copy(buf_ref.at[first + n, rows], ref.at[rows], sems.at[first + n, t])
                )
                copies[-1].start()

    write(keys_ref, 0, (dk_ref, dv_ref))
    for m, ref in enumerate(tile_refs):
        tiles_ref[me ^ m] = ref[...]
    write(tiles_ref, 2, (dq_ref, att_ref))
    for copy in copies:
        copy.wait()


def attend(table_ref, kv_ref, acc_ref, repeat, items):
    blocks = kv_ref.shape[0] // BLOCK
    group = lax.axis_index("ctx") // (repeat * GROUP_HEADS)
    globals_at = table_ref.shape[0] - GLOBALS
    low = lax.broadcasted_iota(jnp.int32, (BLOCK, PAIR), 1) < HEAD_DIM
    place = lax.broadcasted_iota(jnp.int32, (1, SPAN), 1)

    def load(i, qc):
        ids = [jnp.maximum(i - 1, 0), i, jnp.minimum(i + 1, blocks - 1)]
        ids += [table_ref[globals_at + n] for n in range(GLOBALS)]
        ids += [table_ref[(group * ROUNDS + n) * blocks + i] for n in range(ROUNDS)]
        rows = [pl.ds(pl.multiple_of(one * BLOCK, BLOCK), BLOCK) for one in ids]
        kv = jnp.concatenate([kv_ref[r, :] for r in rows], axis=0)
        zero = jnp.zeros_like(qc)
        return rows, kv, jnp.where(low, qc, zero), jnp.where(low, zero, qc)

    def products(kv, q_part, c_part):
        return lax.dot_general(
            jnp.concatenate((q_part, c_part), axis=0),
            kv,
            (((1,), (1,)), ((), ())),
            preferred_element_type=jnp.float32,
        )

    def softmax(i, both):
        absent = ((place < BLOCK) & (i == 0)) | (
            (place >= 2 * BLOCK) & (place < 3 * BLOCK) & (i == blocks - 1)
        )
        scores = jnp.where(absent, NEG_FILL, both[:BLOCK])
        dprob = both[BLOCK:]
        row_max = jnp.max(scores, axis=-1, keepdims=True)
        weights = jnp.exp2((scores - row_max) * EXP_SCALE)
        inverse = 1.0 / jnp.sum(weights, axis=-1, keepdims=True)
        row_dot = jnp.sum(weights * dprob, axis=-1, keepdims=True) * inverse
        probs = weights * inverse
        dscore = probs * (dprob - row_dot)
        return jnp.concatenate((probs.astype(jnp.bfloat16), dscore.astype(jnp.bfloat16)), axis=0)

    def query_side(kv, pd):
        res = jnp.dot(pd, kv, preferred_element_type=jnp.float32)
        return jnp.where(low, res[BLOCK:] * SCALE, res[:BLOCK]).astype(jnp.bfloat16)

    def key_side(q_part, c_part, pd):
        return lax.dot_general(
            pd,
            jnp.concatenate((c_part, q_part), axis=0),
            (((0,), (0,)), ((), ())),
            preferred_element_type=jnp.float32,
        )

    loaded = [load(i, qc) for i, qc, _ in items]
    both = [products(*one[1:]) for one in loaded]
    pds = [softmax(item[0], one) for item, one in zip(items, both)]
    terms = []
    for (_, kv, q_part, c_part), pd, item in zip(loaded, pds, items):
        item[2](query_side(kv, pd))
        terms.append(key_side(q_part, c_part, pd))
    for one, term in zip(loaded, terms):
        for n, r in enumerate(one[0]):
            acc_ref[r, :] += term[n * BLOCK : (n + 1) * BLOCK]


def attend_tiles(repeat, first, table_ref, kv_ref, acc_ref, qc_refs, out_refs):
    per_device = qc_refs[0].shape[0] // BLOCK
    items = []
    for m, (qc_ref, out_ref) in enumerate(zip(qc_refs, out_refs)):
        source = lax.axis_index("ctx") ^ (first + m)
        for local in range(per_device):
            rows = pl.ds(local * BLOCK, BLOCK)

            def put(value, out_ref=out_ref, rows=rows):
                out_ref[rows, :] = value

            items.append((source * per_device + local, qc_ref, rows, put))
    for start in range(0, len(items), UNROLL):
        now = [(i, ref[rows, :], put) for i, ref, rows, put in items[start : start + UNROLL]]
        attend(table_ref, kv_ref, acc_ref, repeat, now)


def part_kernel(repeat, first, size, table_ref, kv_ref, *rest):
    acc_in_refs, rest = rest[: first > 0], rest[first > 0 :]
    qc_refs, acc_ref, out_refs = rest[:size], rest[size], rest[size + 1 :]
    acc_ref[...] = acc_in_refs[0][...] if first else jnp.zeros_like(acc_ref)
    attend_tiles(repeat, first, table_ref, kv_ref, acc_ref, qc_refs, out_refs)


def last_kernel(repeat, first, size, table_ref, kv_ref, acc_in_ref, *rest):
    qc_refs, keys_ref, out_refs = rest[:size], rest[size], rest[size + 1 : -3]
    acc_ref, tile_ref, sems = rest[-3:]
    tokens = qc_refs[0].shape[0]
    acc_ref[...] = acc_in_ref[...]
    attend_tiles(repeat, first, table_ref, kv_ref, acc_ref, qc_refs, out_refs)

    copies = []
    for d in range(keys_ref.shape[0]):
        acc = acc_ref[pl.ds(d * tokens, tokens), :]
        left = lax.broadcasted_iota(jnp.int32, acc.shape, 1) < HEAD_DIM
        tile_ref[d] = jnp.where(left, acc * SCALE, acc).astype(jnp.bfloat16)
        copies.append(pltpu.make_async_copy(tile_ref.at[d], keys_ref.at[d], sems.at[d]))
        copies[-1].start()
    for copy in copies:
        copy.wait()


def per_device(query, key, value, cotangent, global_ids, rand_owner, rand_local):
    tokens, features = query.shape
    heads = features // HEAD_DIM
    devices = lax.axis_size("ctx")
    repeat = max(1, devices // heads)
    count = devices // 2
    params = pltpu.CompilerParams(vmem_limit_bytes=24 << 20)
    roomy = pltpu.CompilerParams(vmem_limit_bytes=60 << 20)
    tile = jax.ShapeDtypeStruct((tokens, PAIR), jnp.bfloat16)

    packed = pl.pallas_call(
        functools.partial(pack_keys_kernel, repeat),
        out_shape=jax.ShapeDtypeStruct((devices, tokens, PAIR), jnp.bfloat16),
        in_specs=[HBM] * 2,
        out_specs=HBM,
        scratch_shapes=[
            pltpu.VMEM((2, tokens, features), jnp.bfloat16),
            pltpu.VMEM((devices, tokens, PAIR), jnp.bfloat16),
            pltpu.SemaphoreType.DMA((2, CHUNKS)),
            pltpu.SemaphoreType.DMA((CHUNKS,)),
        ],
        compiler_params=roomy,
    )(key, value)
    keys = lax.all_to_all(packed, "ctx", 0, 0, tiled=True).reshape(devices * tokens, PAIR)

    def swap(array, mask):
        return lax.ppermute(array, "ctx", [(i, i ^ mask) for i in range(devices)])

    def pack_queries(far, waits):
        return pl.pallas_call(
            functools.partial(pack_queries_kernel, repeat, count, far, len(waits)),
            out_shape=[tile] * count,
            in_specs=[HBM] * 2 + [pl.BlockSpec(memory_space=pl.ANY)] * len(waits),
            out_specs=[HBM] * count,
            scratch_shapes=[
                pltpu.VMEM((2, tokens, features // 2), jnp.bfloat16),
                pltpu.VMEM((count, tokens, PAIR), jnp.bfloat16),
                pltpu.SemaphoreType.DMA((2,)),
                pltpu.SemaphoreType.DMA((count,)),
            ],
            compiler_params=pltpu.CompilerParams(vmem_limit_bytes=16 << 20),
        )(query, cotangent, *waits)

    near_qc = pack_queries(0, [])
    near_qc = [one if m == 0 else swap(one, m) for m, one in enumerate(near_qc)]
    far_qc = pack_queries(1, [])
    far_qc = [swap(one, count + m) for m, one in enumerate(far_qc)]

    picked = (rand_owner * (tokens // BLOCK) + rand_local).T.reshape(-1)
    table = jnp.concatenate((picked, global_ids))
    total = jax.ShapeDtypeStruct((devices * tokens, PAIR), jnp.float32)
    *sizes, last = [devices * part // sum(PARTS) for part in PARTS]
    qc = near_qc + far_qc
    acc, done = [], []
    for size in sizes:
        first = len(done)
        outs = pl.pallas_call(
            functools.partial(part_kernel, repeat, first, size),
            out_shape=[total] + [tile] * size,
            in_specs=[SMEM] + [VMEM] * (1 + len(acc) + size),
            out_specs=[VMEM] * (1 + size),
            compiler_params=params,
            cost_estimate=pl.CostEstimate(flops=size * 10**9, bytes_accessed=4 << 20, transcendentals=0),
        )(table, keys, *acc, *qc[first : first + size])
        acc = [outs[0]]
        done += outs[1:]
    first = len(done)
    keys_out, *outs = pl.pallas_call(
        functools.partial(last_kernel, repeat, first, last),
        out_shape=[jax.ShapeDtypeStruct((devices, tokens, PAIR), jnp.bfloat16)] + [tile] * last,
        in_specs=[SMEM] + [VMEM] * (2 + last),
        out_specs=[HBM] + [VMEM] * last,
        scratch_shapes=[
            pltpu.VMEM((devices * tokens, PAIR), jnp.float32),
            pltpu.VMEM((devices, tokens, PAIR), jnp.bfloat16),
            pltpu.SemaphoreType.DMA((devices,)),
        ],
        compiler_params=params,
    )(table, keys, *acc, *qc[first:])
    back = lax.all_to_all(keys_out, "ctx", 0, 0, tiled=True)
    split = count + EARLY * devices // sum(PARTS)
    early = [swap(one, count + m) for m, one in enumerate(done[count:split])]
    held = done[1:count] + done[split:] + outs
    held = pl.pallas_call(
        functools.partial(hold_kernel, len(held)),
        out_shape=[tile] * len(held),
        in_specs=[VMEM] * len(held) + [pl.BlockSpec(memory_space=pl.ANY)] * len(early),
        out_specs=[VMEM] * len(held),
        compiler_params=params,
        cost_estimate=pl.CostEstimate(flops=10**11, bytes_accessed=1 << 20, transcendentals=0),
    )(*held, *early)
    masks = list(range(1, count)) + list(range(split, devices))
    held = [swap(one, mask) for one, mask in zip(held, masks)]
    tiles = done[:1] + held[: count - 1] + early + held[count - 1 :]
    return pl.pallas_call(
        functools.partial(unpack_kernel, repeat),
        out_shape=[jax.ShapeDtypeStruct((tokens, features), jnp.bfloat16)] * 4,
        in_specs=[VMEM] * (1 + devices),
        out_specs=[HBM] * 4,
        scratch_shapes=[
            pltpu.VMEM((devices, tokens, PAIR), jnp.bfloat16),
            pltpu.VMEM((4, tokens, features), jnp.bfloat16),
            pltpu.SemaphoreType.DMA((4, CHUNKS)),
        ],
        compiler_params=params,
    )(back, *tiles)


def solution(mesh):
    split = P(("groups", "ctx"), None)
    return jax.shard_map(
        per_device,
        mesh=mesh,
        in_specs=(split, split, split, split, P("groups"), P("groups", None), P("groups", None)),
        out_specs=(split, split, split, split),
        check_vma=False,
    )
```
